512 devices in a mesh: dp: 16 (over y, x_lo, core), tensor: 32 (over x_hi, z).
Axes of the slice: x: 4 (x_hi: 2, x_lo: 2; x = x_hi * 2 + x_lo), y: 4, z: 16, core: 2. Of those that a mesh axis runs over, the one named last changes fastest.
Arguments:
- hidden_pre: bfloat16 [2048, 24576], P('dp', 'tensor'), may hold values from -6 to 6
- out_grad: bfloat16 [2048, 6144], P('dp', 'tensor'), may hold values from -0.890625 to 0.890625
- down_weight: bfloat16 [24576, 6144], P('tensor', 'dp'), may hold values from -0.078125 to 0.078125
Outputs:
- grad_hidden: bfloat16 [2048, 24576], P('dp', 'tensor')
- grad_weight: bfloat16 [24576, 6144], P('tensor', 'dp')
The draws below stay inside these ranges and needn't reach their ends.
All inputs are finite; a program needn't handle non-finite values.
Results may differ from the reference program's by a relative error of at most 0.019.
Values may be sent and summed in bfloat16 or wider, within the bound.
A program may use at most 64 MiB of HBM per device.

```python
import math
import jax
import jax.numpy as jnp
from jax import lax

D = 6144
FF = 24576
TOKENS = 2048
N_DP = 16


def shard_levels(key, shape, pieces, least, high):
    gain, own = 1.0, jax.random.fold_in(key, 6)
    for axis_at, shards_of in pieces:
        draws = jnp.exp(jax.random.uniform(jax.random.fold_in(own, axis_at), (shards_of,), jnp.float32, least / len(pieces), high / len(pieces)))
        gain = gain * jnp.repeat(draws, shape[axis_at] // shards_of).reshape([-1 if axis == axis_at else 1 for axis in range(len(shape))])
    return gain


def noise(key, extent, spread, bound, shards=(), held_as=jnp.bfloat16):
    result = jax.random.normal(key, extent, jnp.float32) * spread
    if len(shards) > 0:
        result = shard_levels(key, extent, shards, -0.22, 0.18) * result
    return jnp.clip(result, min=-bound, max=bound).astype(held_as)


def setup_inputs(seed: int = 0) -> dict:
    streams_of = jax.random.split(jax.random.key(seed), 4)
    return {
        "hidden_pre": noise(streams_of[0], (TOKENS, FF), 1.0, 6.0, ((0, 16), (1, 32))),
        "out_grad": noise(streams_of[1], (TOKENS, D), (TOKENS ** -0.25), 0.890625, ((0, 16), (1, 32))),
        "down_weight": noise(streams_of[2], (FF, D), D ** -0.5, 0.078125, ((0, 32), (1, 16))),
    }


coef = math.sqrt(2.0 / math.pi)

def gelu_parts(value):
    inner = coef * (value + 0.044715 * value * value * value)
    tval = jnp.tanh(inner)
    act = 0.5 * value * (1.0 + tval)
    slope = 0.5 * (1.0 + tval) + 0.5 * value * (1.0 - tval * tval) * coef * (1.0 + 3.0 * 0.044715 * value * value)
    return (act, slope)

def reference(hidden_pre, out_grad, down_weight):
    pre = hidden_pre.astype(jnp.float32)
    act, slope = gelu_parts(pre)
    activated = act.astype(jnp.bfloat16)
    width = D // N_DP
    summed = jnp.zeros((TOKENS, FF), jnp.float32)
    for block in range(N_DP):
        cols = out_grad[:, block * width:(block + 1) * width]
        rows = down_weight[:, block * width:(block + 1) * width]
        partial_k = lax.dot_general(cols, rows, (((1,), (1,)), ((), ())), preferred_element_type=jnp.float32)
        summed = summed + partial_k.astype(jnp.bfloat16).astype(jnp.float32)
    grad_hidden = (slope * summed).astype(jnp.bfloat16)
    grad_weight = lax.dot_general(activated, out_grad, (((0,), (0,)), ((), ())), preferred_element_type=jnp.float32)
    return (grad_hidden, grad_weight.astype(jnp.bfloat16))
```

```python
import math

import jax
import jax.numpy as jnp
from jax import lax
from jax.experimental import pallas as pl
from jax.experimental.pallas import tpu as pltpu
from jax.sharding import PartitionSpec as P

coef = math.sqrt(2.0 / math.pi)
MESH = pl.DeviceIdType.MESH
NY, NX, NZ = 4, 2, 16
NQ = NY * NX


def gelu_parts(value):
    inner = coef * (value + 0.044715 * value * value * value)
    tval = jnp.tanh(inner)
    act = 0.5 * value * (1.0 + tval)
    slope = 0.5 * (1.0 + tval) + 0.5 * value * (1.0 - tval * tval) * coef * (
        1.0 + 3.0 * 0.044715 * value * value
    )
    return (act, slope)


def kernel(
    hid_hbm, grad_hbm, w_hbm, gh_ref, gw_ref,
    hid, wts, cols, cols_sib, act_own, act_sib, slope, stage, parts,
    loc_sem, w_sem, g_send, g_recv, right_send, right_recv, left_send, left_recv,
    gs_send, gs_recv, ax_sem, ay_send, ay_recv, ah_send, ah_recv, as_send, as_recv,
    rs_send, rs_recv,
):
    rem, div = lax.rem, lax.div
    dp = lax.axis_index("dp")
    tn = lax.axis_index("tensor")
    core, chip = rem(dp, 2), div(dp, 2)
    cy, cx = div(chip, NX), rem(chip, NX)
    cz, ch = rem(tn, NZ), div(tn, NZ)
    sib = dp + 1 - 2 * core

    def chip_at(y, x):
        return rem(y, NY) * NX + rem(x, NX)

    def block_at(j):
        return chip_at(cy + div(j, NX), cx + rem(j, NX))

    def at(dp_to, tn_to):
        return (dp_to, tn_to)

    def slot_at(place):
        j = div(place, 2)
        return block_at(j), rem(place, 2)

    to_chip, to_half, to_part = div(tn, 4), rem(div(tn, 2), 2), rem(tn, 2)
    to_j = rem(cy - div(to_chip, NX) + NY, NY) * NX + rem(cx - rem(to_chip, NX) + NX, NX)
    to_dp = to_chip * 2 + core
    to_z = to_j * 2 + to_half
    my_block, my_half = slot_at(cz)
    from_dp = my_block * 2 + core

    cp_hid = pltpu.make_async_copy(hid_hbm, hid, loc_sem.at[0])
    cp_w = pltpu.make_async_copy(w_hbm, wts.at[core], loc_sem.at[1])
    cp_hid.start()
    cp_w.start()

    barrier = pltpu.get_barrier_semaphore()
    expect = jnp.int32(0)
    for part in range(2):
        from_tn = chip * 4 + my_half * 2 + part
        here = jnp.logical_and(from_dp == dp, from_tn == tn)

        @pl.when(jnp.logical_not(here))
        def _():
            pl.semaphore_signal(barrier, inc=1, device_id=at(from_dp, from_tn), device_id_type=MESH)

    up = ch * NZ + rem(cz + 1, NZ)
    down = ch * NZ + rem(cz + NZ - 1, NZ)
    for other in (up, down):
        pl.semaphore_signal(barrier, inc=1, device_id=at(dp, other), device_id_type=MESH)
    pl.semaphore_signal(barrier, inc=1, device_id=at(sib, tn), device_id_type=MESH)
    for j in range(1, NQ):
        pl.semaphore_signal(barrier, inc=1, device_id=at(block_at(j) * 2 + core, tn), device_id_type=MESH)
    expect = jnp.int32(2 + 1 + NQ - 1)
    for half in range(2):
        away = jnp.logical_or(to_dp != dp, half * NZ + to_z != tn)
        expect = expect + away.astype(jnp.int32)
    pl.semaphore_wait(barrier, expect)

    def g_copy(half):
        return pltpu.make_async_remote_copy(
            src_ref=grad_hbm,
            dst_ref=cols.at[chip, to_half, pl.ds(pl.multiple_of(to_part * 192, 64), 192)],
            send_sem=g_send.at[half], recv_sem=g_recv.at[to_part],
            device_id=at(to_dp, half * NZ + to_z), device_id_type=MESH,
        )

    def g_local(half):
        return pltpu.make_async_copy(
            grad_hbm,
            cols.at[chip, to_half, pl.ds(pl.multiple_of(to_part * 192, 64), 192)],
            g_recv.at[to_part],
        )

    for half in range(2):
        away = jnp.logical_or(to_dp != dp, half * NZ + to_z != tn)

        @pl.when(away)
        def _():
            g_copy(half).start()

        @pl.when(jnp.logical_not(away))
        def _():
            g_local(half).start()

    cp_w.wait()
    w_copy = pltpu.make_async_remote_copy(
        src_ref=wts.at[core], dst_ref=wts.at[core], send_sem=w_sem.at[0], recv_sem=w_sem.at[1],
        device_id=at(sib, tn), device_id_type=MESH,
    )
    w_copy.start()

    cp_hid.wait()
    act, slp = gelu_parts(hid[...].astype(jnp.float32))
    act_own[chip] = act.astype(jnp.bfloat16)
    slope[...] = slp

    started = []

    def send(src, dst, send_sem, recv_sem, dp_to):
        copy = pltpu.make_async_remote_copy(
            src_ref=src, dst_ref=dst, send_sem=send_sem, recv_sem=recv_sem,
            device_id=at(dp_to, tn), device_id_type=MESH,
        )
        copy.start()
        started.append(copy)
        return copy

    def got(dst, recv_sem):
        pltpu.make_async_remote_copy(
            src_ref=dst, dst_ref=dst, send_sem=recv_sem, recv_sem=recv_sem,
            device_id=at(sib, tn), device_id_type=MESH,
        ).wait_recv()

    x_chip = chip_at(cy, cx + 1)

    def act_to_y(x_off, block):
        for k, off in ((0, 1), (1, 3)):
            dest = chip_at(cy + off, cx) * 2 + core
            send(act_own.at[block], act_own.at[block], ay_send.at[x_off, k], ay_recv.at[x_off, k], dest)

    def act_to_sib(j):
        block = block_at(j)
        send(act_own.at[block], act_sib.at[block], as_send.at[j], as_recv.at[j], sib)

    send(act_own.at[chip], act_own.at[chip], ax_sem.at[0], ax_sem.at[1], x_chip * 2 + core)
    act_to_y(0, chip)
    act_to_sib(0)

    def act_from_y(x_off):
        for k, off in ((0, 3), (1, 1)):
            block = chip_at(cy + off, cx + x_off)
            got(act_own.at[block], ay_recv.at[x_off, k])
            rows = pl.ds(k * 64, 64)
            dest = chip_at(cy + (1 if k == 0 else 3), cx) * 2 + core
            send(act_own.at[block, rows], act_own.at[block, rows],
                 ah_send.at[x_off, k], ah_recv.at[x_off, k], dest)
            act_to_sib(off * NX + x_off)

    def act_halves(x_off):
        block = chip_at(cy + 2, cx + x_off)
        for k in range(2):
            got(act_own.at[block, pl.ds(k * 64, 64)], ah_recv.at[x_off, k])
        act_to_sib(2 * NX + x_off)

    for part in range(2):
        got(cols.at[my_block, my_half, pl.ds(part * 192, 192)], g_recv.at[part])

    def ring(place, tn_to, send_sem, recv_sem):
        block, half = slot_at(place)
        copy = pltpu.make_async_remote_copy(
            src_ref=cols.at[block, half], dst_ref=cols.at[block, half],
            send_sem=send_sem, recv_sem=recv_sem, device_id=at(dp, tn_to), device_id_type=MESH,
        )
        copy.start()
        started.append(copy)

    ring(cz, up, right_send.at[0], right_recv.at[0])
    ring(cz, down, left_send.at[0], left_recv.at[0])

    def partial(step):
        odd = rem(cz + step, 2)
        j = div(rem(cz + NZ + jnp.where(odd == 1, step, -step), NZ), 2)
        block = block_at(j)
        send(cols.at[block, 1 - core], cols_sib.at[block], gs_send.at[step - 1], gs_recv.at[block], sib)
        if step == 1:
            w_copy.wait_recv()
        value = jnp.dot(wts[0], cols[block, 0], preferred_element_type=jnp.float32)
        value += jnp.dot(wts[1], cols[block, 1], preferred_element_type=jnp.float32)
        value = value.astype(jnp.bfloat16)
        copy = pltpu.make_async_remote_copy(
            src_ref=stage.at[step - 1], dst_ref=parts.at[chip],
            send_sem=rs_send.at[step - 1], recv_sem=rs_recv.at[chip],
            device_id=at(block * 2 + core, tn), device_id_type=MESH,
        )

        @pl.when(block == chip)
        def _():
            parts[chip] = value

        @pl.when(block != chip)
        def _():
            stage[step - 1] = value
            copy.start()

        return block, copy

    rs = []
    for step in range(1, NZ // 2 + 1):
        place = rem(cz + NZ - step, NZ)
        block, half = slot_at(place)
        got(cols.at[block, half], right_recv.at[step - 1])
        if step < NZ // 2:
            ring(place, up, right_send.at[step], right_recv.at[step])
        if step < NZ // 2:
            place = rem(cz + step, NZ)
            block, half = slot_at(place)
            got(cols.at[block, half], left_recv.at[step - 1])
            if step < NZ // 2 - 1:
                ring(place, down, left_send.at[step], left_recv.at[step])
        rs.append(partial(step))
        if step == 1:
            got(act_own.at[x_chip], ax_sem.at[1])
            act_to_y(1, x_chip)
            act_to_sib(1)
        elif step == 2:
            act_from_y(0)
        elif step == 4:
            act_from_y(1)
        elif step == 5:
            act_halves(0)
        elif step == 7:
            act_halves(1)

    for j in range(NQ):
        got(act_sib.at[block_at(j)], as_recv.at[j])
    for block in range(NQ):
        got(cols_sib.at[block], gs_recv.at[block])
    lhs = jnp.concatenate([cols[block, core] for block in range(NQ)], axis=1)
    total = jnp.dot(lhs, act_own[...].reshape(NQ * 128, 768), preferred_element_type=jnp.float32)
    lhs = jnp.concatenate([cols_sib[block] for block in range(NQ)], axis=1)
    total += jnp.dot(lhs, act_sib[...].reshape(NQ * 128, 768), preferred_element_type=jnp.float32)
    gw_ref[...] = total.astype(jnp.bfloat16)

    for j in range(1, NQ):
        block = block_at(j)
        got(parts.at[block], rs_recv.at[block])
    summed = parts[0].astype(jnp.float32)
    for block in range(1, NQ):
        summed += parts[block].astype(jnp.float32)
    gh_ref[...] = (slope[...] * summed.T).astype(jnp.bfloat16)

    for half in range(2):
        @pl.when(jnp.logical_or(to_dp != dp, half * NZ + to_z != tn))
        def _():
            g_copy(half).wait_send()

    w_copy.wait_send()
    for copy in started:
        copy.wait_send()
    for block, copy in rs:
        @pl.when(block != chip)
        def _():
            copy.wait_send()


def local(hidden_pre, out_grad, down_weight):
    bf16, f32 = jnp.bfloat16, jnp.float32
    dma = pltpu.SemaphoreType.DMA
    half = NZ // 2
    grad_hidden, gw = pl.pallas_call(
        kernel,
        out_shape=(
            jax.ShapeDtypeStruct((128, 768), bf16),
            jax.ShapeDtypeStruct((384, 768), bf16),
        ),
        in_specs=[pl.BlockSpec(memory_space=pl.ANY)] * 3,
        out_specs=[pl.BlockSpec(memory_space=pltpu.VMEM)] * 2,
        scratch_shapes=[
            pltpu.VMEM((128, 768), bf16),
            pltpu.VMEM((2, 768, 384), bf16),
            pltpu.VMEM((NQ, 2, 384, 128), bf16),
            pltpu.VMEM((NQ, 384, 128), bf16),
            pltpu.VMEM((NQ, 128, 768), bf16),
            pltpu.VMEM((NQ, 128, 768), bf16),
            pltpu.VMEM((128, 768), f32),
            pltpu.VMEM((half, 768, 128), bf16),
            pltpu.VMEM((NQ, 768, 128), bf16),
            dma((2,)), dma((2,)), dma((2,)), dma((2,)),
            dma((half,)), dma((half,)), dma((half,)), dma((half,)),
            dma((half,)), dma((NQ,)), dma((2,)), dma((2, 2)), dma((2, 2)),
            dma((2, 2)), dma((2, 2)), dma((NQ,)), dma((NQ,)),
            dma((half,)), dma((NQ,)),
        ],
        compiler_params=pltpu.CompilerParams(
            collective_id=0, has_side_effects=True, vmem_limit_bytes=48 * 1024 * 1024
        ),
    )(hidden_pre, out_grad.T, down_weight)
    return (grad_hidden, gw.T)


def solution(mesh):
    placed = (P("dp", "tensor"), P("dp", "tensor"), P("tensor", "dp"))
    return jax.shard_map(
        local,
        mesh=mesh,
        in_specs=placed,
        out_specs=(P("dp", "tensor"), P("tensor", "dp")),
        check_vma=False,
    )
```

```python
import math

import jax
import jax.numpy as jnp
from jax import lax
from jax.experimental import pallas as pl
from jax.experimental.pallas import tpu as pltpu
from jax.sharding import PartitionSpec as P

coef = math.sqrt(2.0 / math.pi)
MESH = pl.DeviceIdType.MESH
NY, NX, NZ = 4, 2, 16
NQ = NY * NX


def gelu_parts(value):
    inner = coef * (value + 0.044715 * value * value * value)
    tval = jnp.tanh(inner)
    act = 0.5 * value * (1.0 + tval)
    slope = 0.5 * (1.0 + tval) + 0.5 * value * (1.0 - tval * tval) * coef * (
        1.0 + 3.0 * 0.044715 * value * value
    )
    return (act, slope)


def kernel(
    hid_hbm, grad_hbm, w_hbm, gh_ref, gw_ref,
    hid, wts, cols, cols_sib, act_own, act_sib, slope, first, second, comb, x_parts, y_parts,
    loc_sem, w_sem, g_sem, peer_sem, right_send, right_recv, left_send, left_recv,
    gs_send, gs_recv, ax_sem, ay_send, ay_recv, ah_send, ah_recv, as_send, as_recv,
    x_send, x_recv, y_send, y_recv,
):
    rem, div = lax.rem, lax.div
    dp = lax.axis_index("dp")
    tn = lax.axis_index("tensor")
    core, chip = rem(dp, 2), div(dp, 2)
    cy, cx = div(chip, NX), rem(chip, NX)
    cz, ch = rem(tn, NZ), div(tn, NZ)
    sib = dp + 1 - 2 * core

    def chip_at(dy, dx):
        return rem(cy + dy, NY) * NX + rem(cx + dx, NX)

    def block_at(j):
        return chip_at(div(j, NX), rem(j, NX))

    def at(dp_to, tn_to):
        return (dp_to, tn_to)

    def peer_at(dy, dx):
        return at(chip_at(dy, dx) * 2 + core, tn)

    def slot_at(place):
        return block_at(div(place, 2)), rem(place, 2)

    def piece(place, part):
        block, half = slot_at(place)
        return cols.at[block, half, pl.ds(pl.multiple_of(part * 192, 64), 192)]

    to_chip, to_half, to_part = div(tn, 4), rem(div(tn, 2), 2), rem(tn, 2)
    to_j = rem(cy - div(to_chip, NX) + NY, NY) * NX + rem(cx - rem(to_chip, NX) + NX, NX)
    to_dp = to_chip * 2 + core
    to_tn = to_part * NZ + to_j * 2 + to_half
    from_dp = slot_at(cz)[0] * 2 + core
    from_tn = chip * 4 + rem(cz, 2) * 2 + ch
    to_away = jnp.logical_or(to_dp != dp, to_tn != tn)
    from_away = jnp.logical_or(from_dp != dp, from_tn != tn)

    lead = div(cz, 4)
    turn = 1 - 2 * rem(div(cz, 2), 2)
    order = [lead, rem(lead + NY - turn, NY), rem(lead + NY + turn, NY), rem(lead + 2, NY)]
    last = order[3]

    up = at(dp, ch * NZ + rem(cz + 1, NZ))
    down = at(dp, ch * NZ + rem(cz + NZ - 1, NZ))
    across = at(dp, rem(tn + NZ, 2 * NZ))
    beside = at(sib, tn)

    barrier = pltpu.get_barrier_semaphore()
    greet = [up, down, across, beside, peer_at(0, 1), peer_at(NY - last, 1)]
    greet += [peer_at(dy, 0) for dy in range(1, NY)]
    for other in greet:
        pl.semaphore_signal(barrier, inc=1, device_id=other, device_id_type=MESH)

    @pl.when(from_away)
    def _():
        pl.semaphore_signal(barrier, inc=1, device_id=at(from_dp, from_tn), device_id_type=MESH)

    cp_hid = pltpu.make_async_copy(hid_hbm, hid, loc_sem.at[0])
    cp_w = pltpu.make_async_copy(w_hbm, wts.at[core], loc_sem.at[1])
    cp_hid.start()
    cp_w.start()
    cp_hid.wait()
    act, slp = gelu_parts(hid[...].astype(jnp.float32))
    act_own[chip] = act.astype(jnp.bfloat16)
    slope[...] = slp
    cp_w.wait()
    pl.semaphore_wait(barrier, len(greet) + to_away.astype(jnp.int32))

    started = []

    def send(src, dst, send_sem, recv_sem, dest, keep=True):
        copy = pltpu.make_async_remote_copy(
            src_ref=src, dst_ref=dst, send_sem=send_sem, recv_sem=recv_sem,
            device_id=dest, device_id_type=MESH,
        )
        copy.start()
        if keep:
            started.append(copy)

    def got(dst, recv_sem):
        pltpu.make_async_remote_copy(
            src_ref=dst, dst_ref=dst, send_sem=recv_sem, recv_sem=recv_sem,
            device_id=beside, device_id_type=MESH,
        ).wait_recv()

    def sent(src, send_sem):
        pltpu.make_async_remote_copy(
            src_ref=src, dst_ref=src, send_sem=send_sem, recv_sem=send_sem,
            device_id=beside, device_id_type=MESH,
        ).wait_send()

    g_dst = cols.at[chip, to_half, pl.ds(pl.multiple_of(to_part * 192, 64), 192)]

    @pl.when(to_away)
    def _():
        send(grad_hbm, g_dst, g_sem.at[0], g_sem.at[1], at(to_dp, to_tn), keep=False)

    @pl.when(jnp.logical_not(to_away))
    def _():
        pltpu.make_async_copy(grad_hbm, g_dst, g_sem.at[1]).start()

    def act_to_y(dx):
        block = chip_at(0, dx)
        for k, dy in ((0, 1), (1, NY - 1)):
            send(act_own.at[block], act_own.at[block], ay_send.at[dx, k], ay_recv.at[dx, k], peer_at(dy, 0))

    def act_to_sib(j):
        block = block_at(j)
        send(act_own.at[block], act_sib.at[block], as_send.at[j], as_recv.at[j], beside)

    def act_from_y(dx):
        for k, dy in ((0, NY - 1), (1, 1)):
            block = chip_at(dy, dx)
            got(act_own.at[block], ay_recv.at[dx, k])
            rows = pl.ds(k * 64, 64)
            send(act_own.at[block, rows], act_own.at[block, rows],
                 ah_send.at[dx, k], ah_recv.at[dx, k], peer_at(NY - dy, 0))
            act_to_sib(dy * NX + dx)

    def act_halves(dx):
        block = chip_at(2, dx)
        for k in range(2):
            got(act_own.at[block, pl.ds(k * 64, 64)], ah_recv.at[dx, k])
        act_to_sib(2 * NX + dx)

    send(wts.at[core], wts.at[core], w_sem.at[0], w_sem.at[1], beside)
    send(act_own.at[chip], act_own.at[chip], ax_sem.at[0], ax_sem.at[1], peer_at(0, 1))
    act_to_y(0)
    act_to_sib(0)

    pieces = (ch, 1 - ch)

    def right(step, n):
        ref = piece(rem(cz + NZ - step, NZ), pieces[n])
        if step > 0:
            got(ref, right_recv.at[n, step - 1])
        if step < NZ // 2:
            send(ref, ref, right_send.at[n, step], right_recv.at[n, step], up)

    def left(step, n):
        ref = piece(rem(cz + step, NZ), pieces[n])
        if step > 0:
            got(ref, left_recv.at[n, step - 1])
        if step < NZ // 2 - 1:
            send(ref, ref, left_send.at[n, step], left_recv.at[n, step], down)

    got(piece(cz, ch), g_sem.at[1])
    right(0, 0)
    left(0, 0)
    send(piece(cz, ch), piece(cz, ch), peer_sem.at[0], peer_sem.at[1], across)
    got(piece(cz, 1 - ch), peer_sem.at[1])
    right(0, 1)
    left(0, 1)

    def partial(step):
        odd = rem(cz + step, 2)
        j = div(rem(cz + NZ + jnp.where(odd == 1, step, -step), NZ), 2)
        dy, dx = div(j, NX), rem(j, NX)
        block = block_at(j)
        send(cols.at[block, 1 - core], cols_sib.at[block], gs_send.at[step - 1], gs_recv.at[block], beside)
        if step == 1:
            got(wts.at[1 - core], w_sem.at[1])
        value = jnp.dot(wts[0], cols[block, 0], preferred_element_type=jnp.float32)
        value += jnp.dot(wts[1], cols[block, 1], preferred_element_type=jnp.float32)
        value = value.astype(jnp.bfloat16)
        final = (dy == last).astype(jnp.int32)

        @pl.when(dx == 1)
        def _():
            second[dy] = value
            send(second.at[dy], x_parts.at[dy], x_send.at[dy], x_recv.at[dy], peer_at(final * dy, 1), keep=False)

        @pl.when(jnp.logical_and(dx == 0, jnp.logical_or(final == 0, dy != 0)))
        def _():
            first[dy] = value

        @pl.when(jnp.logical_and(jnp.logical_and(dx == 0, final == 1), dy != 0))
        def _():
            send(first.at[dy], y_parts.at[dy], y_send.at[dy], y_recv.at[dy], peer_at(dy, 0), keep=False)

        @pl.when(jnp.logical_and(jnp.logical_and(dx == 0, final == 1), dy == 0))
        def _():
            y_parts[0] = value

    def combine(i):
        dy = order[i]
        got(x_parts.at[dy], x_recv.at[dy])
        value = (first[dy].astype(jnp.float32) + x_parts[dy].astype(jnp.float32)).astype(jnp.bfloat16)

        @pl.when(dy == 0)
        def _():
            y_parts[0] = value

        @pl.when(dy != 0)
        def _():
            comb[i] = value
            send(comb.at[i], y_parts.at[dy], y_send.at[dy], y_recv.at[dy], peer_at(dy, 0), keep=False)

    for step in range(1, NZ // 2 + 1):
        for n in range(2):
            right(step, n)
            if step < NZ // 2:
                left(step, n)
        partial(step)
        if step == 1:
            got(act_own.at[chip_at(0, 1)], ax_sem.at[1])
            act_to_y(1)
            act_to_sib(1)
        elif step == 2:
            act_from_y(0)
        elif step == 4:
            combine(0)
            act_from_y(1)
        elif step == 5:
            act_halves(0)
        elif step == 6:
            combine(1)
        elif step == 7:
            act_halves(1)
        elif step == 8:
            combine(2)

    lhs = jnp.concatenate([cols[block, core] for block in range(NQ)], axis=1)
    total = jnp.dot(lhs, act_own[...].reshape(NQ * 128, 768), preferred_element_type=jnp.float32)
    for j in range(NQ):
        got(act_sib.at[block_at(j)], as_recv.at[j])
    for block in range(NQ):
        got(cols_sib.at[block], gs_recv.at[block])
    lhs = jnp.concatenate([cols_sib[block] for block in range(NQ)], axis=1)
    total += jnp.dot(lhs, act_sib[...].reshape(NQ * 128, 768), preferred_element_type=jnp.float32)
    gw_ref[...] = total.astype(jnp.bfloat16)

    for dy in range(1, NY):
        got(y_parts.at[dy], y_recv.at[dy])
    got(x_parts.at[last], x_recv.at[last])
    summed = x_parts[last].astype(jnp.float32)
    for dy in range(NY):
        summed += y_parts[dy].astype(jnp.float32)
    gh_ref[...] = (slope[...] * summed.T).astype(jnp.bfloat16)

    @pl.when(to_away)
    def _():
        sent(grad_hbm, g_sem.at[0])

    for copy in started:
        copy.wait_send()
    for dy in range(NY):
        sent(second.at[dy], x_send.at[dy])
    for dy in range(1, NY):
        sent(comb.at[0], y_send.at[dy])


def local(hidden_pre, out_grad, down_weight):
    bf16, f32 = jnp.bfloat16, jnp.float32
    dma = pltpu.SemaphoreType.DMA
    half = NZ // 2
    grad_hidden, gw = pl.pallas_call(
        kernel,
        out_shape=(
            jax.ShapeDtypeStruct((128, 768), bf16),
            jax.ShapeDtypeStruct((384, 768), bf16),
        ),
        in_specs=[pl.BlockSpec(memory_space=pl.ANY)] * 3,
        out_specs=[pl.BlockSpec(memory_space=pltpu.VMEM)] * 2,
        scratch_shapes=[
            pltpu.VMEM((128, 768), bf16),
            pltpu.VMEM((2, 768, 384), bf16),
            pltpu.VMEM((NQ, 2, 384, 128), bf16),
            pltpu.VMEM((NQ, 384, 128), bf16),
            pltpu.VMEM((NQ, 128, 768), bf16),
            pltpu.VMEM((NQ, 128, 768), bf16),
            pltpu.VMEM((128, 768), f32),
            pltpu.VMEM((NY, 768, 128), bf16),
            pltpu.VMEM((NY, 768, 128), bf16),
            pltpu.VMEM((NY - 1, 768, 128), bf16),
            pltpu.VMEM((NY, 768, 128), bf16),
            pltpu.VMEM((NY, 768, 128), bf16),
            dma((2,)), dma((2,)), dma((2,)), dma((2,)),
            dma((2, half)), dma((2, half)), dma((2, half)), dma((2, half)),
            dma((half,)), dma((NQ,)), dma((2,)), dma((2, 2)), dma((2, 2)),
            dma((2, 2)), dma((2, 2)), dma((NQ,)), dma((NQ,)),
            dma((NY,)), dma((NY,)), dma((NY,)), dma((NY,)),
        ],
        compiler_params=pltpu.CompilerParams(
            collective_id=0, has_side_effects=True, vmem_limit_bytes=60 * 1024 * 1024
        ),
    )(hidden_pre, out_grad.T, down_weight)
    return (grad_hidden, gw.T)


def solution(mesh):
    placed = (P("dp", "tensor"), P("dp", "tensor"), P("tensor", "dp"))
    return jax.shard_map(
        local,
        mesh=mesh,
        in_specs=placed,
        out_specs=(P("dp", "tensor"), P("tensor", "dp")),
        check_vma=False,
    )
```

```python
import math

import jax
import jax.numpy as jnp
from jax import lax
from jax.experimental import pallas as pl
from jax.experimental.pallas import tpu as pltpu
from jax.sharding import PartitionSpec as P

coef = math.sqrt(2.0 / math.pi)
MESH = pl.DeviceIdType.MESH
NY, NX, NZ = 4, 2, 16
NQ = NY * NX


def gelu_parts(value):
    inner = coef * (value + 0.044715 * value * value * value)
    tval = jnp.tanh(inner)
    act = 0.5 * value * (1.0 + tval)
    slope = 0.5 * (1.0 + tval) + 0.5 * value * (1.0 - tval * tval) * coef * (
        1.0 + 3.0 * 0.044715 * value * value
    )
    return (act, slope)


def kernel(
    hid_hbm, grad_hbm, w_hbm, gh_ref, gw_ref,
    hid, wts, cols, act_own, act_sib, slope, first, second, comb, x_parts, y_parts,
    loc_sem, w_sem, g_send, g_recv, peer_send, peer_recv, hand_send, hand_recv, right_send, right_recv, left_send, left_recv,
    gs_send, gs_recv, ax_sem, ay_send, ay_recv, ah_send, ah_recv, as_send, as_recv,
    x_send, x_recv, y_send, y_recv,
):
    rem, div = lax.rem, lax.div
    dp = lax.axis_index("dp")
    tn = lax.axis_index("tensor")
    core, chip = rem(dp, 2), div(dp, 2)
    cy, cx = div(chip, NX), rem(chip, NX)
    cz, ch = rem(tn, NZ), div(tn, NZ)
    sib = dp + 1 - 2 * core

    def chip_at(dy, dx):
        return rem(cy + dy, NY) * NX + rem(cx + dx, NX)

    def block_at(j):
        return chip_at(div(j, NX), rem(j, NX))

    def at(dp_to, tn_to):
        return (dp_to, tn_to)

    def peer_at(dy, dx):
        return at(chip_at(dy, dx) * 2 + core, tn)

    def slot_at(place):
        return block_at(div(place, 2)), rem(place, 2)

    def piece(par, place, part):
        block, half = slot_at(place)
        return cols.at[par, block, half, pl.ds(pl.multiple_of(part * 192, 64), 192)]

    to_chip, to_half, to_part = div(tn, 4), rem(div(tn, 2), 2), rem(tn, 2)
    to_j = rem(cy - div(to_chip, NX) + NY, NY) * NX + rem(cx - rem(to_chip, NX) + NX, NX)
    to_dp = to_chip * 2 + 1
    to_tn = to_part * NZ + to_j * 2 + to_half
    from_dp = slot_at(cz)[0] * 2
    from_tn = chip * 4 + rem(cz, 2) * 2 + ch
    to_away = jnp.logical_or(to_dp != dp, to_tn != tn)

    lead = div(cz, 4)
    turn = 1 - 2 * rem(div(cz, 2), 2)
    order = [lead, rem(lead + NY - turn, NY), rem(lead + NY + turn, NY), rem(lead + 2, NY)]
    last = order[3]

    up = at(dp, ch * NZ + rem(cz + 1, NZ))
    down = at(dp, ch * NZ + rem(cz + NZ - 1, NZ))
    across = at(dp, rem(tn + NZ, 2 * NZ))
    beside = at(sib, tn)

    barrier = pltpu.get_barrier_semaphore()
    greet = [beside, peer_at(0, 1), peer_at(NY - last, 1)]
    greet += [peer_at(dy, 0) for dy in range(1, NY)]
    for other in greet:
        pl.semaphore_signal(barrier, inc=1, device_id=other, device_id_type=MESH)

    @pl.when(core == 1)
    def _():
        for other in (up, down, across, at(from_dp, from_tn)):
            pl.semaphore_signal(barrier, inc=1, device_id=other, device_id_type=MESH)

        @pl.when(jnp.logical_or(from_dp + 1 != dp, from_tn != tn))
        def _():
            pl.semaphore_signal(barrier, inc=1, device_id=at(from_dp + 1, from_tn), device_id_type=MESH)

    cp_hid = pltpu.make_async_copy(hid_hbm, hid, loc_sem.at[0])
    cp_w = pltpu.make_async_copy(w_hbm, wts.at[core], loc_sem.at[1])
    cp_hid.start()
    cp_w.start()
    cp_hid.wait()
    act, slp = gelu_parts(hid[...].astype(jnp.float32))
    act_own[chip] = act.astype(jnp.bfloat16)
    slope[...] = slp
    cp_w.wait()
    pl.semaphore_wait(barrier, len(greet) + 3 * core + to_away.astype(jnp.int32))

    started = []

    def send(src, dst, send_sem, recv_sem, dest, keep=True):
        copy = pltpu.make_async_remote_copy(
            src_ref=src, dst_ref=dst, send_sem=send_sem, recv_sem=recv_sem,
            device_id=dest, device_id_type=MESH,
        )
        copy.start()
        if keep:
            started.append(copy)

    def got(dst, recv_sem):
        pltpu.make_async_remote_copy(
            src_ref=dst, dst_ref=dst, send_sem=recv_sem, recv_sem=recv_sem,
            device_id=beside, device_id_type=MESH,
        ).wait_recv()

    def sent(src, send_sem):
        pltpu.make_async_remote_copy(
            src_ref=src, dst_ref=src, send_sem=send_sem, recv_sem=send_sem,
            device_id=beside, device_id_type=MESH,
        ).wait_send()

    g_dst = cols.at[core, chip, to_half, pl.ds(pl.multiple_of(to_part * 192, 64), 192)]

    @pl.when(to_away)
    def _():
        send(grad_hbm, g_dst, g_send, g_recv.at[core], at(to_dp, to_tn), keep=False)

    @pl.when(jnp.logical_not(to_away))
    def _():
        pltpu.make_async_copy(grad_hbm, g_dst, g_recv.at[core]).start()

    def act_to_y(dx):
        block = chip_at(0, dx)
        for k, dy in ((0, 1), (1, NY - 1)):
            send(act_own.at[block], act_own.at[block], ay_send.at[dx, k], ay_recv.at[dx, k], peer_at(dy, 0))

    def act_to_sib(j):
        block = block_at(j)
        send(act_own.at[block], act_sib.at[block], as_send.at[j], as_recv.at[j], beside)

    def act_from_y(dx):
        for k, dy in ((0, NY - 1), (1, 1)):
            block = chip_at(dy, dx)
            got(act_own.at[block], ay_recv.at[dx, k])
            rows = pl.ds(k * 64, 64)
            send(act_own.at[block, rows], act_own.at[block, rows],
                 ah_send.at[dx, k], ah_recv.at[dx, k], peer_at(NY - dy, 0))
            act_to_sib(dy * NX + dx)

    def act_halves(dx):
        block = chip_at(2, dx)
        for k in range(2):
            got(act_own.at[block, pl.ds(k * 64, 64)], ah_recv.at[dx, k])
        act_to_sib(2 * NX + dx)

    send(wts.at[core], wts.at[core], w_sem.at[0], w_sem.at[1], beside)
    send(act_own.at[chip], act_own.at[chip], ax_sem.at[0], ax_sem.at[1], peer_at(0, 1))
    act_to_y(0)
    act_to_sib(0)

    pieces = (ch, 1 - ch)

    def right(step, n, par):
        ref = piece(par, rem(cz + NZ - step, NZ), pieces[n])
        if step > 0:
            got(ref, right_recv.at[par, n, step - 1])
        if step < NZ // 2:
            send(ref, ref, right_send.at[par, n, step], right_recv.at[par, n, step], up, keep=False)

    def left(step, n, par):
        ref = piece(par, rem(cz + step, NZ), pieces[n])
        if step > 0:
            got(ref, left_recv.at[par, n, step - 1])
        if step < NZ // 2 - 1:
            send(ref, ref, left_send.at[par, n, step], left_recv.at[par, n, step], down, keep=False)

    def hand(way, step):
        block, half = slot_at(rem(cz + NZ + (step if way else -step), NZ))
        ref = cols.at[0, block, half]
        send(ref, ref, hand_send.at[way, step], hand_recv.at[way, step], beside, keep=False)

    def handed(way, step):
        block, half = slot_at(rem(cz + NZ + (step if way else -step), NZ))
        got(cols.at[0, block, half], hand_recv.at[way, step])

    def ring(step):
        @pl.when(core == 1)
        def _():
            for n in range(2):
                for par in range(2):
                    right(step, n, par)
                    if step < NZ // 2:
                        left(step, n, par)
            hand(0, step)
            if step < NZ // 2:
                hand(1, step)

        @pl.when(core == 0)
        def _():
            handed(0, step)
            if step < NZ // 2:
                handed(1, step)

    @pl.when(core == 1)
    def _():
        for par in range(2):
            ref = piece(par, cz, ch)
            got(ref, g_recv.at[par])
            right(0, 0, par)
            left(0, 0, par)
            send(ref, ref, peer_send.at[par], peer_recv.at[par], across, keep=False)
        for par in range(2):
            got(piece(par, cz, 1 - ch), peer_recv.at[par])
            right(0, 1, par)
            left(0, 1, par)
        hand(0, 0)

    @pl.when(core == 0)
    def _():
        handed(0, 0)

    def partial(step):
        odd = rem(cz + step, 2)
        j = div(rem(cz + NZ + jnp.where(odd == 1, step, -step), NZ), 2)
        dy, dx = div(j, NX), rem(j, NX)
        block = block_at(j)

        @pl.when(core == 1)
        def _():
            ref = cols.at[1, block, 0]
            send(ref, ref, gs_send.at[step - 1], gs_recv.at[block], beside, keep=False)

        if step == 1:
            got(wts.at[1 - core], w_sem.at[1])
        value = jnp.dot(wts[0], cols[core, block, 0], preferred_element_type=jnp.float32)
        value += jnp.dot(wts[1], cols[core, block, 1], preferred_element_type=jnp.float32)
        value = value.astype(jnp.bfloat16)
        final = (dy == last).astype(jnp.int32)

        @pl.when(dx == 1)
        def _():
            second[dy] = value
            send(second.at[dy], x_parts.at[dy], x_send.at[dy], x_recv.at[dy], peer_at(final * dy, 1), keep=False)

        @pl.when(jnp.logical_and(dx == 0, jnp.logical_or(final == 0, dy != 0)))
        def _():
            first[dy] = value

        @pl.when(jnp.logical_and(jnp.logical_and(dx == 0, final == 1), dy != 0))
        def _():
            send(first.at[dy], y_parts.at[dy], y_send.at[dy], y_recv.at[dy], peer_at(dy, 0), keep=False)

        @pl.when(jnp.logical_and(jnp.logical_and(dx == 0, final == 1), dy == 0))
        def _():
            y_parts[0] = value

    def combine(i):
        dy = order[i]
        got(x_parts.at[dy], x_recv.at[dy])
        value = (first[dy].astype(jnp.float32) + x_parts[dy].astype(jnp.float32)).astype(jnp.bfloat16)

        @pl.when(dy == 0)
        def _():
            y_parts[0] = value

        @pl.when(dy != 0)
        def _():
            comb[i] = value
            send(comb.at[i], y_parts.at[dy], y_send.at[dy], y_recv.at[dy], peer_at(dy, 0), keep=False)

    for step in range(1, NZ // 2 + 1):
        ring(step)
        partial(step)
        if step == 1:
            got(act_own.at[chip_at(0, 1)], ax_sem.at[1])
            act_to_y(1)
            act_to_sib(1)
        elif step == 2:
            act_from_y(0)
        elif step == 4:
            combine(0)
            act_from_y(1)
        elif step == 5:
            act_halves(0)
        elif step == 6:
            combine(1)
        elif step == 7:
            act_halves(1)
        elif step == 8:
            combine(2)

    lhs = jnp.concatenate([cols[core, block, core] for block in range(NQ)], axis=1)
    total = jnp.dot(lhs, act_own[...].reshape(NQ * 128, 768), preferred_element_type=jnp.float32)
    for j in range(NQ):
        got(act_sib.at[block_at(j)], as_recv.at[j])

    @pl.when(core == 0)
    def _():
        for block in range(NQ):
            got(cols.at[1, block, 0], gs_recv.at[block])

    lhs = jnp.concatenate([cols[1 - core, block, core] for block in range(NQ)], axis=1)
    total += jnp.dot(lhs, act_sib[...].reshape(NQ * 128, 768), preferred_element_type=jnp.float32)
    gw_ref[...] = total.astype(jnp.bfloat16)

    for dy in range(1, NY):
        got(y_parts.at[dy], y_recv.at[dy])
    got(x_parts.at[last], x_recv.at[last])
    summed = x_parts[last].astype(jnp.float32)
    for dy in range(NY):
        summed += y_parts[dy].astype(jnp.float32)
    gh_ref[...] = (slope[...] * summed.T).astype(jnp.bfloat16)

    @pl.when(to_away)
    def _():
        sent(grad_hbm, g_send)

    @pl.when(core == 1)
    def _():
        ref = piece(0, cz, 0)
        for par in range(2):
            sent(ref, peer_send.at[par])
            for n in range(2):
                for step in range(NZ // 2):
                    sent(ref, right_send.at[par, n, step])
                    if step < NZ // 2 - 1:
                        sent(ref, left_send.at[par, n, step])
        whole = cols.at[0, 0, 0]
        for step in range(NZ // 2 + 1):
            sent(whole, hand_send.at[0, step])
            if 0 < step < NZ // 2:
                sent(whole, hand_send.at[1, step])
        for step in range(NZ // 2):
            sent(whole, gs_send.at[step])

    for copy in started:
        copy.wait_send()
    for dy in range(NY):
        sent(second.at[dy], x_send.at[dy])
    for dy in range(1, NY):
        sent(comb.at[0], y_send.at[dy])


def local(hidden_pre, out_grad, down_weight):
    bf16, f32 = jnp.bfloat16, jnp.float32
    dma = pltpu.SemaphoreType.DMA
    half = NZ // 2
    grad_hidden, gw = pl.pallas_call(
        kernel,
        out_shape=(
            jax.ShapeDtypeStruct((128, 768), bf16),
            jax.ShapeDtypeStruct((384, 768), bf16),
        ),
        in_specs=[pl.BlockSpec(memory_space=pl.ANY)] * 3,
        out_specs=[pl.BlockSpec(memory_space=pltpu.VMEM)] * 2,
        scratch_shapes=[
            pltpu.VMEM((128, 768), bf16),
            pltpu.VMEM((2, 768, 384), bf16),
            pltpu.VMEM((2, NQ, 2, 384, 128), bf16),
            pltpu.VMEM((NQ, 128, 768), bf16),
            pltpu.VMEM((NQ, 128, 768), bf16),
            pltpu.VMEM((128, 768), f32),
            pltpu.VMEM((NY, 768, 128), bf16),
            pltpu.VMEM((NY, 768, 128), bf16),
            pltpu.VMEM((NY - 1, 768, 128), bf16),
            pltpu.VMEM((NY, 768, 128), bf16),
            pltpu.VMEM((NY, 768, 128), bf16),
            dma((2,)), dma((2,)), dma, dma((2,)), dma((2,)), dma((2,)),
            dma((2, half + 1)), dma((2, half + 1)),
            dma((2, 2, half)), dma((2, 2, half)), dma((2, 2, half)), dma((2, 2, half)),
            dma((half,)), dma((NQ,)), dma((2,)), dma((2, 2)), dma((2, 2)),
            dma((2, 2)), dma((2, 2)), dma((NQ,)), dma((NQ,)),
            dma((NY,)), dma((NY,)), dma((NY,)), dma((NY,)),
        ],
        compiler_params=pltpu.CompilerParams(
            collective_id=0, has_side_effects=True, vmem_limit_bytes=60 * 1024 * 1024
        ),
    )(hidden_pre, out_grad.T, down_weight)
    return (grad_hidden, gw.T)


def solution(mesh):
    placed = (P("dp", "tensor"), P("dp", "tensor"), P("tensor", "dp"))
    return jax.shard_map(
        local,
        mesh=mesh,
        in_specs=placed,
        out_specs=(P("dp", "tensor"), P("tensor", "dp")),
        check_vma=False,
    )
```

```python
import math

import jax
import jax.numpy as jnp
from jax import lax
from jax.experimental import pallas as pl
from jax.experimental.pallas import tpu as pltpu
from jax.sharding import PartitionSpec as P

coef = math.sqrt(2.0 / math.pi)
MESH = pl.DeviceIdType.MESH
NY, NX, NZ = 4, 2, 16
NQ = NY * NX


def gelu_parts(value):
    inner = coef * (value + 0.044715 * value * value * value)
    tval = jnp.tanh(inner)
    act = 0.5 * value * (1.0 + tval)
    slope = 0.5 * (1.0 + tval) + 0.5 * value * (1.0 - tval * tval) * coef * (
        1.0 + 3.0 * 0.044715 * value * value
    )
    return (act, slope)


def kernel(
    hid_hbm, grad_hbm, w_hbm, gh_ref, gw_ref,
    hid, wts, cols, act_own, act_sib, slope, stage, parts,
    loc_sem, w_sem, g_send, g_recv, peer_send, peer_recv, hand_send, hand_recv, right_send, right_recv, left_send, left_recv,
    gs_send, gs_recv, ax_sem, ay_send, ay_recv, ah_send, ah_recv, as_send, as_recv,
    rs_send, rs_recv,
):
    rem, div = lax.rem, lax.div
    dp = lax.axis_index("dp")
    tn = lax.axis_index("tensor")
    core, chip = rem(dp, 2), div(dp, 2)
    cy, cx = div(chip, NX), rem(chip, NX)
    cz, ch = rem(tn, NZ), div(tn, NZ)
    sib = dp + 1 - 2 * core

    def chip_at(dy, dx):
        return rem(cy + dy, NY) * NX + rem(cx + dx, NX)

    def block_at(j):
        return chip_at(div(j, NX), rem(j, NX))

    def at(dp_to, tn_to):
        return (dp_to, tn_to)

    def peer_at(dy, dx):
        return at(chip_at(dy, dx) * 2 + core, tn)

    def slot_at(place):
        return block_at(div(place, 2)), rem(place, 2)

    def piece(par, place, part):
        block, half = slot_at(place)
        return cols.at[par, block, half, pl.ds(pl.multiple_of(part * 192, 64), 192)]

    to_chip, to_half, to_part = div(tn, 4), rem(div(tn, 2), 2), rem(tn, 2)
    to_j = rem(cy - div(to_chip, NX) + NY, NY) * NX + rem(cx - rem(to_chip, NX) + NX, NX)
    to_dp = to_chip * 2 + 1
    to_tn = to_part * NZ + to_j * 2 + to_half
    from_dp = slot_at(cz)[0] * 2
    from_tn = chip * 4 + rem(cz, 2) * 2 + ch
    to_away = jnp.logical_or(to_dp != dp, to_tn != tn)

    up = at(dp, ch * NZ + rem(cz + 1, NZ))
    down = at(dp, ch * NZ + rem(cz + NZ - 1, NZ))
    across = at(dp, rem(tn + NZ, 2 * NZ))
    beside = at(sib, tn)

    barrier = pltpu.get_barrier_semaphore()
    greet = [beside] + [peer_at(j // NX, j % NX) for j in range(1, NQ)]
    for other in greet:
        pl.semaphore_signal(barrier, inc=1, device_id=other, device_id_type=MESH)

    @pl.when(core == 1)
    def _():
        for other in (up, down, across, at(from_dp, from_tn)):
            pl.semaphore_signal(barrier, inc=1, device_id=other, device_id_type=MESH)

        @pl.when(jnp.logical_or(from_dp + 1 != dp, from_tn != tn))
        def _():
            pl.semaphore_signal(barrier, inc=1, device_id=at(from_dp + 1, from_tn), device_id_type=MESH)

    cp_hid = pltpu.make_async_copy(hid_hbm, hid, loc_sem.at[0])
    cp_w = pltpu.make_async_copy(w_hbm, wts.at[core], loc_sem.at[1])
    cp_hid.start()
    cp_w.start()
    pl.semaphore_wait(barrier, len(greet) + 3 * core + to_away.astype(jnp.int32))

    started = []

    def send(src, dst, send_sem, recv_sem, dest, keep=True):
        copy = pltpu.make_async_remote_copy(
            src_ref=src, dst_ref=dst, send_sem=send_sem, recv_sem=recv_sem,
            device_id=dest, device_id_type=MESH,
        )
        copy.start()
        if keep:
            started.append(copy)

    def got(dst, recv_sem):
        pltpu.make_async_remote_copy(
            src_ref=dst, dst_ref=dst, send_sem=recv_sem, recv_sem=recv_sem,
            device_id=beside, device_id_type=MESH,
        ).wait_recv()

    def sent(src, send_sem):
        pltpu.make_async_remote_copy(
            src_ref=src, dst_ref=src, send_sem=send_sem, recv_sem=send_sem,
            device_id=beside, device_id_type=MESH,
        ).wait_send()

    g_dst = cols.at[core, chip, to_half, pl.ds(pl.multiple_of(to_part * 192, 64), 192)]

    @pl.when(to_away)
    def _():
        send(grad_hbm, g_dst, g_send, g_recv.at[core], at(to_dp, to_tn), keep=False)

    @pl.when(jnp.logical_not(to_away))
    def _():
        pltpu.make_async_copy(grad_hbm, g_dst, g_recv.at[core]).start()

    def act_to_y(dx):
        block = chip_at(0, dx)
        for k, dy in ((0, 1), (1, NY - 1)):
            send(act_own.at[block], act_own.at[block], ay_send.at[dx, k], ay_recv.at[dx, k], peer_at(dy, 0))

    def act_to_sib(j):
        block = block_at(j)
        send(act_own.at[block], act_sib.at[block], as_send.at[j], as_recv.at[j], beside)

    def act_from_y(dx):
        for k, dy in ((0, NY - 1), (1, 1)):
            block = chip_at(dy, dx)
            got(act_own.at[block], ay_recv.at[dx, k])
            rows = pl.ds(k * 64, 64)
            send(act_own.at[block, rows], act_own.at[block, rows],
                 ah_send.at[dx, k], ah_recv.at[dx, k], peer_at(NY - dy, 0))
            act_to_sib(dy * NX + dx)

    def act_halves(dx):
        block = chip_at(2, dx)
        for k in range(2):
            got(act_own.at[block, pl.ds(k * 64, 64)], ah_recv.at[dx, k])
        act_to_sib(2 * NX + dx)

    cp_w.wait()
    send(wts.at[core], wts.at[core], w_sem.at[0], w_sem.at[1], beside)
    cp_hid.wait()
    act, slp = gelu_parts(hid[...].astype(jnp.float32))
    act_own[chip] = act.astype(jnp.bfloat16)
    slope[...] = slp
    send(act_own.at[chip], act_own.at[chip], ax_sem.at[0], ax_sem.at[1], peer_at(0, 1))
    act_to_y(0)
    act_to_sib(0)

    pieces = (ch, 1 - ch)

    def right(step, n, par):
        ref = piece(par, rem(cz + NZ - step, NZ), pieces[n])
        if step > 0:
            got(ref, right_recv.at[par, n, step - 1])
        if step < NZ // 2:
            send(ref, ref, right_send.at[par, n, step], right_recv.at[par, n, step], up, keep=False)

    def left(step, n, par):
        ref = piece(par, rem(cz + step, NZ), pieces[n])
        if step > 0:
            got(ref, left_recv.at[par, n, step - 1])
        if step < NZ // 2 - 1:
            send(ref, ref, left_send.at[par, n, step], left_recv.at[par, n, step], down, keep=False)

    def hand(way, step):
        block, half = slot_at(rem(cz + NZ + (step if way else -step), NZ))
        ref = cols.at[0, block, half]
        send(ref, ref, hand_send.at[way, step], hand_recv.at[way, step], beside, keep=False)

    def handed(way, step):
        block, half = slot_at(rem(cz + NZ + (step if way else -step), NZ))
        got(cols.at[0, block, half], hand_recv.at[way, step])

    def ring(step):
        @pl.when(core == 1)
        def _():
            for n in range(2):
                for par in range(2):
                    right(step, n, par)
                    if step < NZ // 2:
                        left(step, n, par)
            hand(0, step)
            if step < NZ // 2:
                hand(1, step)

        @pl.when(core == 0)
        def _():
            handed(0, step)
            if step < NZ // 2:
                handed(1, step)

    @pl.when(core == 1)
    def _():
        for par in range(2):
            ref = piece(par, cz, ch)
            got(ref, g_recv.at[par])
            right(0, 0, par)
            left(0, 0, par)
            send(ref, ref, peer_send.at[par], peer_recv.at[par], across, keep=False)
        for par in range(2):
            got(piece(par, cz, 1 - ch), peer_recv.at[par])
            right(0, 1, par)
            left(0, 1, par)
        hand(0, 0)

    @pl.when(core == 0)
    def _():
        handed(0, 0)

    def partial(step):
        odd = rem(cz + step, 2)
        j = div(rem(cz + NZ + jnp.where(odd == 1, step, -step), NZ), 2)
        dy, dx = div(j, NX), rem(j, NX)
        block = block_at(j)

        @pl.when(core == 1)
        def _():
            ref = cols.at[1, block, 0]
            send(ref, ref, gs_send.at[step - 1], gs_recv.at[block], beside, keep=False)

        if step == 1:
            got(wts.at[1 - core], w_sem.at[1])
        value = jnp.dot(wts[0], cols[core, block, 0], preferred_element_type=jnp.float32)
        value += jnp.dot(wts[1], cols[core, block, 1], preferred_element_type=jnp.float32)
        value = value.astype(jnp.bfloat16)

        @pl.when(j == 0)
        def _():
            parts[0] = value

        @pl.when(j != 0)
        def _():
            stage[step - 1] = value
            send(stage.at[step - 1], parts.at[j], rs_send.at[j], rs_recv.at[j], peer_at(dy, dx), keep=False)

    for step in range(1, NZ // 2 + 1):
        ring(step)
        partial(step)
        if step == 1:
            got(act_own.at[chip_at(0, 1)], ax_sem.at[1])
            act_to_y(1)
            act_to_sib(1)
        elif step == 2:
            act_from_y(0)
        elif step == 4:
            act_from_y(1)
        elif step == 5:
            act_halves(0)
        elif step == 7:
            act_halves(1)

    lhs = jnp.concatenate([cols[core, block, core] for block in range(NQ)], axis=1)
    total = jnp.dot(lhs, act_own[...].reshape(NQ * 128, 768), preferred_element_type=jnp.float32)
    for j in range(NQ):
        got(act_sib.at[block_at(j)], as_recv.at[j])

    @pl.when(core == 0)
    def _():
        for block in range(NQ):
            got(cols.at[1, block, 0], gs_recv.at[block])

    lhs = jnp.concatenate([cols[1 - core, block, core] for block in range(NQ)], axis=1)
    total += jnp.dot(lhs, act_sib[...].reshape(NQ * 128, 768), preferred_element_type=jnp.float32)
    gw_ref[...] = total.astype(jnp.bfloat16)

    for j in range(1, NQ):
        got(parts.at[j], rs_recv.at[j])
    summed = parts[0].astype(jnp.float32)
    for j in range(1, NQ):
        summed += parts[j].astype(jnp.float32)
    gh_ref[...] = (slope[...] * summed.T).astype(jnp.bfloat16)

    @pl.when(to_away)
    def _():
        sent(grad_hbm, g_send)

    @pl.when(core == 1)
    def _():
        ref = piece(0, cz, 0)
        for par in range(2):
            sent(ref, peer_send.at[par])
            for n in range(2):
                for step in range(NZ // 2):
                    sent(ref, right_send.at[par, n, step])
                    if step < NZ // 2 - 1:
                        sent(ref, left_send.at[par, n, step])
        whole = cols.at[0, 0, 0]
        for step in range(NZ // 2 + 1):
            sent(whole, hand_send.at[0, step])
            if 0 < step < NZ // 2:
                sent(whole, hand_send.at[1, step])
        for step in range(NZ // 2):
            sent(whole, gs_send.at[step])

    for copy in started:
        copy.wait_send()
    for j in range(1, NQ):
        sent(stage.at[0], rs_send.at[j])


def local(hidden_pre, out_grad, down_weight):
    bf16, f32 = jnp.bfloat16, jnp.float32
    dma = pltpu.SemaphoreType.DMA
    half = NZ // 2
    grad_hidden, gw = pl.pallas_call(
        kernel,
        out_shape=(
            jax.ShapeDtypeStruct((128, 768), bf16),
            jax.ShapeDtypeStruct((384, 768), bf16),
        ),
        in_specs=[pl.BlockSpec(memory_space=pl.ANY)] * 3,
        out_specs=[pl.BlockSpec(memory_space=pltpu.VMEM)] * 2,
        scratch_shapes=[
            pltpu.VMEM((128, 768), bf16),
            pltpu.VMEM((2, 768, 384), bf16),
            pltpu.VMEM((2, NQ, 2, 384, 128), bf16),
            pltpu.VMEM((NQ, 128, 768), bf16),
            pltpu.VMEM((NQ, 128, 768), bf16),
            pltpu.VMEM((128, 768), f32),
            pltpu.VMEM((NQ, 768, 128), bf16),
            pltpu.VMEM((NQ, 768, 128), bf16),
            dma((2,)), dma((2,)), dma, dma((2,)), dma((2,)), dma((2,)),
            dma((2, half + 1)), dma((2, half + 1)),
            dma((2, 2, half)), dma((2, 2, half)), dma((2, 2, half)), dma((2, 2, half)),
            dma((half,)), dma((NQ,)), dma((2,)), dma((2, 2)), dma((2, 2)),
            dma((2, 2)), dma((2, 2)), dma((NQ,)), dma((NQ,)),
            dma((NQ,)), dma((NQ,)),
        ],
        compiler_params=pltpu.CompilerParams(
            collective_id=0, has_side_effects=True, vmem_limit_bytes=60 * 1024 * 1024
        ),
    )(hidden_pre, out_grad.T, down_weight)
    return (grad_hidden, gw.T)


def solution(mesh):
    placed = (P("dp", "tensor"), P("dp", "tensor"), P("tensor", "dp"))
    return jax.shard_map(
        local,
        mesh=mesh,
        in_specs=placed,
        out_specs=(P("dp", "tensor"), P("tensor", "dp")),
        check_vma=False,
    )
```

```python
import math

import jax
import jax.numpy as jnp
from jax import lax
from jax.experimental import pallas as pl
from jax.experimental.pallas import tpu as pltpu
from jax.sharding import PartitionSpec as P

coef = math.sqrt(2.0 / math.pi)
MESH = pl.DeviceIdType.MESH
NY, NX, NZ = 4, 2, 16
NQ = NY * NX


def gelu_parts(value):
    inner = coef * (value + 0.044715 * value * value * value)
    tval = jnp.tanh(inner)
    act = 0.5 * value * (1.0 + tval)
    slope = 0.5 * (1.0 + tval) + 0.5 * value * (1.0 - tval * tval) * coef * (
        1.0 + 3.0 * 0.044715 * value * value
    )
    return (act, slope)


def kernel(
    hid_hbm, grad_hbm, w_hbm, gh_ref, gw_ref,
    hid, wts, cols, act_own, act_sib, slope, stage, parts,
    loc_sem, w_sem, g_send, g_recv, peer_send, peer_recv, hand_send, hand_recv, right_send, right_recv, left_send, left_recv,
    gs_send, gs_recv, ax_sem, ay_send, ay_recv, ah_send, ah_recv, as_send, as_recv,
    rs_send, rs_recv,
):
    rem, div = lax.rem, lax.div
    dp = lax.axis_index("dp")
    tn = lax.axis_index("tensor")
    core, chip = rem(dp, 2), div(dp, 2)
    cy, cx = div(chip, NX), rem(chip, NX)
    cz, ch = rem(tn, NZ), div(tn, NZ)
    sib = dp + 1 - 2 * core

    def chip_at(dy, dx):
        return rem(cy + dy, NY) * NX + rem(cx + dx, NX)

    def block_at(j):
        return chip_at(div(j, NX), rem(j, NX))

    def at(dp_to, tn_to):
        return (dp_to, tn_to)

    def peer_at(dy, dx):
        return at(chip_at(dy, dx) * 2 + core, tn)

    def shift(j, par):
        return rem(div(j, NX) + 2 * par, NY), rem(j + par, NX)

    def slot_at(place, par):
        return chip_at(*shift(div(place, 2), par)), rem(place, 2)

    def piece(par, place, part):
        block, half = slot_at(place, par)
        return cols.at[par, block, half, pl.ds(pl.multiple_of(part * 192, 64), 192)]

    to_chip, to_half, to_part = div(tn, 4), rem(div(tn, 2), 2), rem(tn, 2)
    to_j = rem(cy - div(to_chip, NX) + NY + 2 * core, NY) * NX + rem(cx - rem(to_chip, NX) + NX + core, NX)
    to_dp = to_chip * 2 + 1
    to_tn = to_part * NZ + to_j * 2 + to_half
    from_dp = [slot_at(cz, par)[0] * 2 + par for par in range(2)]
    from_tn = chip * 4 + rem(cz, 2) * 2 + ch
    to_away = jnp.logical_or(to_dp != dp, to_tn != tn)

    up = at(dp, ch * NZ + rem(cz + 1, NZ))
    down = at(dp, ch * NZ + rem(cz + NZ - 1, NZ))
    across = at(dp, rem(tn + NZ, 2 * NZ))
    beside = at(sib, tn)

    barrier = pltpu.get_barrier_semaphore()
    greet = [beside] + [peer_at(j // NX, j % NX) for j in range(1, NQ)]
    for other in greet:
        pl.semaphore_signal(barrier, inc=1, device_id=other, device_id_type=MESH)

    @pl.when(core == 1)
    def _():
        for other in (up, down, across, at(from_dp[0], from_tn)):
            pl.semaphore_signal(barrier, inc=1, device_id=other, device_id_type=MESH)

        @pl.when(jnp.logical_or(from_dp[1] != dp, from_tn != tn))
        def _():
            pl.semaphore_signal(barrier, inc=1, device_id=at(from_dp[1], from_tn), device_id_type=MESH)

    cp_hid = pltpu.make_async_copy(hid_hbm, hid, loc_sem.at[0])
    cp_w = pltpu.make_async_copy(w_hbm, wts.at[core], loc_sem.at[1])
    cp_hid.start()
    cp_w.start()
    pl.semaphore_wait(barrier, len(greet) + 3 * core + to_away.astype(jnp.int32))

    started = []

    def send(src, dst, send_sem, recv_sem, dest, keep=True):
        copy = pltpu.make_async_remote_copy(
            src_ref=src, dst_ref=dst, send_sem=send_sem, recv_sem=recv_sem,
            device_id=dest, device_id_type=MESH,
        )
        copy.start()
        if keep:
            started.append(copy)

    def got(dst, recv_sem):
        pltpu.make_async_remote_copy(
            src_ref=dst, dst_ref=dst, send_sem=recv_sem, recv_sem=recv_sem,
            device_id=beside, device_id_type=MESH,
        ).wait_recv()

    def sent(src, send_sem):
        pltpu.make_async_remote_copy(
            src_ref=src, dst_ref=src, send_sem=send_sem, recv_sem=send_sem,
            device_id=beside, device_id_type=MESH,
        ).wait_send()

    g_dst = cols.at[core, chip, to_half, pl.ds(pl.multiple_of(to_part * 192, 64), 192)]

    @pl.when(to_away)
    def _():
        send(grad_hbm, g_dst, g_send, g_recv.at[core], at(to_dp, to_tn), keep=False)

    @pl.when(jnp.logical_not(to_away))
    def _():
        pltpu.make_async_copy(grad_hbm, g_dst, g_recv.at[core]).start()

    def act_to_y(dx):
        block = chip_at(0, dx)
        for k, dy in ((0, 1), (1, NY - 1)):
            send(act_own.at[block], act_own.at[block], ay_send.at[dx, k], ay_recv.at[dx, k], peer_at(dy, 0))

    def act_to_sib(j):
        block = block_at(j)
        send(act_own.at[block], act_sib.at[block], as_send.at[j], as_recv.at[j], beside)

    def act_from_y(dx):
        for k, dy in ((0, NY - 1), (1, 1)):
            block = chip_at(dy, dx)
            got(act_own.at[block], ay_recv.at[dx, k])
            rows = pl.ds(k * 64, 64)
            send(act_own.at[block, rows], act_own.at[block, rows],
                 ah_send.at[dx, k], ah_recv.at[dx, k], peer_at(NY - dy, 0))
            act_to_sib(dy * NX + dx)

    def act_halves(dx):
        block = chip_at(2, dx)
        for k in range(2):
            got(act_own.at[block, pl.ds(k * 64, 64)], ah_recv.at[dx, k])
        act_to_sib(2 * NX + dx)

    cp_w.wait()
    send(wts.at[core], wts.at[core], w_sem.at[0], w_sem.at[1], beside)
    cp_hid.wait()
    act, slp = gelu_parts(hid[...].astype(jnp.float32))
    act_own[chip] = act.astype(jnp.bfloat16)
    slope[...] = slp
    send(act_own.at[chip], act_own.at[chip], ax_sem.at[0], ax_sem.at[1], peer_at(0, 1))
    act_to_y(0)
    act_to_sib(0)

    pieces = (ch, 1 - ch)

    def right(step, n, par):
        ref = piece(par, rem(cz + NZ - step, NZ), pieces[n])
        if step > 0:
            got(ref, right_recv.at[par, n, step - 1])
        if step < NZ // 2:
            send(ref, ref, right_send.at[par, n, step], right_recv.at[par, n, step], up, keep=False)

    def left(step, n, par):
        ref = piece(par, rem(cz + step, NZ), pieces[n])
        if step > 0:
            got(ref, left_recv.at[par, n, step - 1])
        if step < NZ // 2 - 1:
            send(ref, ref, left_send.at[par, n, step], left_recv.at[par, n, step], down, keep=False)

    def hand(way, step):
        block, half = slot_at(rem(cz + NZ + (step if way else -step), NZ), 0)
        ref = cols.at[0, block, half]
        send(ref, ref, hand_send.at[way, step], hand_recv.at[way, step], beside, keep=False)

    def handed(way, step):
        block, half = slot_at(rem(cz + NZ + (step if way else -step), NZ), 0)
        got(cols.at[0, block, half], hand_recv.at[way, step])

    def ring(step):
        @pl.when(core == 1)
        def _():
            for n in range(2):
                for par in range(2):
                    right(step, n, par)
                    if step < NZ // 2:
                        left(step, n, par)
            hand(0, step)
            if step < NZ // 2:
                hand(1, step)

        @pl.when(core == 0)
        def _():
            handed(0, step)
            if step < NZ // 2:
                handed(1, step)

    got(act_own.at[chip_at(0, 1)], ax_sem.at[1])
    act_to_y(1)
    act_to_sib(1)
    act_from_y(0)

    @pl.when(core == 1)
    def _():
        for par in range(2):
            ref = piece(par, cz, ch)
            got(ref, g_recv.at[par])
            right(0, 0, par)
            left(0, 0, par)
            send(ref, ref, peer_send.at[par], peer_recv.at[par], across, keep=False)
        for par in range(2):
            got(piece(par, cz, 1 - ch), peer_recv.at[par])
            right(0, 1, par)
            left(0, 1, par)
        hand(0, 0)

    @pl.when(core == 0)
    def _():
        handed(0, 0)

    def partial(step):
        odd = rem(cz + step, 2)
        j = div(rem(cz + NZ + jnp.where(odd == 1, step, -step), NZ), 2)
        dy, dx = shift(j, core)
        block = chip_at(dy, dx)
        j = dy * NX + dx

        @pl.when(core == 1)
        def _():
            ref = cols.at[1, block, 0]
            send(ref, ref, gs_send.at[step - 1], gs_recv.at[block], beside, keep=False)

        if step == 1:
            got(wts.at[1 - core], w_sem.at[1])
        value = jnp.dot(wts[0], cols[core, block, 0], preferred_element_type=jnp.float32)
        value += jnp.dot(wts[1], cols[core, block, 1], preferred_element_type=jnp.float32)
        value = value.astype(jnp.bfloat16)

        @pl.when(j == 0)
        def _():
            parts[0] = value

        @pl.when(j != 0)
        def _():
            stage[step - 1] = value
            send(stage.at[step - 1], parts.at[j], rs_send.at[j], rs_recv.at[j], peer_at(dy, dx), keep=False)

    for step in range(1, NZ // 2 + 1):
        ring(step)
        partial(step)
        if step == 1:
            act_from_y(1)
        elif step == 2:
            act_halves(0)
        elif step == 3:
            act_halves(1)

    lhs = jnp.concatenate([cols[core, block, core] for block in range(NQ)], axis=1)
    total = jnp.dot(lhs, act_own[...].reshape(NQ * 128, 768), preferred_element_type=jnp.float32)
    for j in range(NQ):
        got(act_sib.at[block_at(j)], as_recv.at[j])

    @pl.when(core == 0)
    def _():
        for block in range(NQ):
            got(cols.at[1, block, 0], gs_recv.at[block])

    lhs = jnp.concatenate([cols[1 - core, block, core] for block in range(NQ)], axis=1)
    total += jnp.dot(lhs, act_sib[...].reshape(NQ * 128, 768), preferred_element_type=jnp.float32)
    gw_ref[...] = total.astype(jnp.bfloat16)

    for j in range(1, NQ):
        got(parts.at[j], rs_recv.at[j])
    summed = parts[0].astype(jnp.float32)
    for j in range(1, NQ):
        summed += parts[j].astype(jnp.float32)
    gh_ref[...] = (slope[...] * summed.T).astype(jnp.bfloat16)

    @pl.when(to_away)
    def _():
        sent(grad_hbm, g_send)

    @pl.when(core == 1)
    def _():
        ref = piece(0, cz, 0)
        for par in range(2):
            sent(ref, peer_send.at[par])
            for n in range(2):
                for step in range(NZ // 2):
                    sent(ref, right_send.at[par, n, step])
                    if step < NZ // 2 - 1:
                        sent(ref, left_send.at[par, n, step])
        whole = cols.at[0, 0, 0]
        for step in range(NZ // 2 + 1):
            sent(whole, hand_send.at[0, step])
            if 0 < step < NZ // 2:
                sent(whole, hand_send.at[1, step])
        for step in range(NZ // 2):
            sent(whole, gs_send.at[step])

    for copy in started:
        copy.wait_send()
    for j in range(1, NQ):
        sent(stage.at[0], rs_send.at[j])


def local(hidden_pre, out_grad, down_weight):
    bf16, f32 = jnp.bfloat16, jnp.float32
    dma = pltpu.SemaphoreType.DMA
    half = NZ // 2
    grad_hidden, gw = pl.pallas_call(
        kernel,
        out_shape=(
            jax.ShapeDtypeStruct((128, 768), bf16),
            jax.ShapeDtypeStruct((384, 768), bf16),
        ),
        in_specs=[pl.BlockSpec(memory_space=pl.ANY)] * 3,
        out_specs=[pl.BlockSpec(memory_space=pltpu.VMEM)] * 2,
        scratch_shapes=[
            pltpu.VMEM((128, 768), bf16),
            pltpu.VMEM((2, 768, 384), bf16),
            pltpu.VMEM((2, NQ, 2, 384, 128), bf16),
            pltpu.VMEM((NQ, 128, 768), bf16),
            pltpu.VMEM((NQ, 128, 768), bf16),
            pltpu.VMEM((128, 768), f32),
            pltpu.VMEM((NQ, 768, 128), bf16),
            pltpu.VMEM((NQ, 768, 128), bf16),
            dma((2,)), dma((2,)), dma, dma((2,)), dma((2,)), dma((2,)),
            dma((2, half + 1)), dma((2, half + 1)),
            dma((2, 2, half)), dma((2, 2, half)), dma((2, 2, half)), dma((2, 2, half)),
            dma((half,)), dma((NQ,)), dma((2,)), dma((2, 2)), dma((2, 2)),
            dma((2, 2)), dma((2, 2)), dma((NQ,)), dma((NQ,)),
            dma((NQ,)), dma((NQ,)),
        ],
        compiler_params=pltpu.CompilerParams(
            collective_id=0, has_side_effects=True, vmem_limit_bytes=60 * 1024 * 1024
        ),
    )(hidden_pre, out_grad.T, down_weight)
    return (grad_hidden, gw.T)


def solution(mesh):
    placed = (P("dp", "tensor"), P("dp", "tensor"), P("tensor", "dp"))
    return jax.shard_map(
        local,
        mesh=mesh,
        in_specs=placed,
        out_specs=(P("dp", "tensor"), P("tensor", "dp")),
        check_vma=False,
    )
```

```python
import math

import jax
import jax.numpy as jnp
from jax import lax
from jax.experimental import pallas as pl
from jax.experimental.pallas import tpu as pltpu
from jax.sharding import PartitionSpec as P

coef = math.sqrt(2.0 / math.pi)
MESH = pl.DeviceIdType.MESH
NY, NX, NZ = 4, 2, 16
NQ = NY * NX


def gelu_parts(value):
    inner = coef * (value + 0.044715 * value * value * value)
    tval = jnp.tanh(inner)
    act = 0.5 * value * (1.0 + tval)
    slope = 0.5 * (1.0 + tval) + 0.5 * value * (1.0 - tval * tval) * coef * (
        1.0 + 3.0 * 0.044715 * value * value
    )
    return (act, slope)


def kernel(
    hid_hbm, grad_hbm, w_hbm, gh_ref, gw_ref,
    hid, wts, cols, acts, slope, stage, parts,
    loc_sem, w_sem, g_send, g_recv, peer_send, peer_recv, hand_send, hand_recv, right_send, right_recv, left_send, left_recv,
    gs_send, gs_recv, own_send, own_recv, ax_sem, ay_send, ay_recv, ah_send, ah_recv, as_send, as_recv,
    rs_send, rs_recv,
):
    rem, div = lax.rem, lax.div
    dp = lax.axis_index("dp")
    tn = lax.axis_index("tensor")
    core, chip = rem(dp, 2), div(dp, 2)
    cy, cx = div(chip, NX), rem(chip, NX)
    cz, ch = rem(tn, NZ), div(tn, NZ)
    sib = dp + 1 - 2 * core

    def chip_at(dy, dx):
        return rem(cy + dy, NY) * NX + rem(cx + dx, NX)

    def block_at(j):
        return chip_at(div(j, NX), rem(j, NX))

    def at(dp_to, tn_to):
        return (dp_to, tn_to)

    def peer_at(dy, dx):
        return at(chip_at(dy, dx) * 2 + core, tn)

    def shift(j, par):
        return rem(div(j, NX) + 2 * par, NY), rem(j + par, NX)

    def slot_at(place, par):
        return chip_at(*shift(div(place, 2), par)), rem(place, 2)

    def piece(par, place, part):
        block, half = slot_at(place, par)
        return cols.at[par, block, half, pl.ds(pl.multiple_of(part * 192, 64), 192)]

    to_chip, to_half, to_part = div(tn, 4), rem(div(tn, 2), 2), rem(tn, 2)
    to_j = rem(cy - div(to_chip, NX) + NY + 2 * core, NY) * NX + rem(cx - rem(to_chip, NX) + NX + core, NX)
    to_dp = to_chip * 2 + 1
    to_tn = to_part * NZ + to_j * 2 + to_half
    from_dp = [slot_at(cz, par)[0] * 2 + par for par in range(2)]
    from_tn = chip * 4 + rem(cz, 2) * 2 + ch
    to_away = jnp.logical_or(to_dp != dp, to_tn != tn)

    up = at(dp, ch * NZ + rem(cz + 1, NZ))
    down = at(dp, ch * NZ + rem(cz + NZ - 1, NZ))
    across = at(dp, rem(tn + NZ, 2 * NZ))
    beside = at(sib, tn)

    barrier = pltpu.get_barrier_semaphore()
    @pl.when(core == 1)
    def _():
        pl.semaphore_signal(barrier, inc=1, device_id=at(from_dp[0], from_tn), device_id_type=MESH)

        @pl.when(jnp.logical_or(from_dp[1] != dp, from_tn != tn))
        def _():
            pl.semaphore_signal(barrier, inc=1, device_id=at(from_dp[1], from_tn), device_id_type=MESH)

        for other in (up, down, across):
            pl.semaphore_signal(barrier, inc=1, device_id=other, device_id_type=MESH)

    greet = [beside] + [peer_at(j // NX, j % NX) for j in range(1, NQ)]
    for other in greet:
        pl.semaphore_signal(barrier, inc=1, device_id=other, device_id_type=MESH)

    cp_hid = pltpu.make_async_copy(hid_hbm, hid, loc_sem.at[0])
    cp_w = pltpu.make_async_copy(w_hbm, wts.at[core], loc_sem.at[1])
    cp_hid.start()
    cp_w.start()
    pl.semaphore_wait(barrier, len(greet) + 3 * core + to_away.astype(jnp.int32))

    started = []

    def send(src, dst, send_sem, recv_sem, dest, keep=True):
        copy = pltpu.make_async_remote_copy(
            src_ref=src, dst_ref=dst, send_sem=send_sem, recv_sem=recv_sem,
            device_id=dest, device_id_type=MESH,
        )
        copy.start()
        if keep:
            started.append(copy)

    def got(dst, recv_sem):
        pltpu.make_async_remote_copy(
            src_ref=dst, dst_ref=dst, send_sem=recv_sem, recv_sem=recv_sem,
            device_id=beside, device_id_type=MESH,
        ).wait_recv()

    def sent(src, send_sem):
        pltpu.make_async_remote_copy(
            src_ref=src, dst_ref=src, send_sem=send_sem, recv_sem=send_sem,
            device_id=beside, device_id_type=MESH,
        ).wait_send()

    g_dst = cols.at[core, chip, to_half, pl.ds(pl.multiple_of(to_part * 192, 64), 192)]

    @pl.when(to_away)
    def _():
        send(grad_hbm, g_dst, g_send, g_recv.at[core], at(to_dp, to_tn), keep=False)

    @pl.when(jnp.logical_not(to_away))
    def _():
        pltpu.make_async_copy(grad_hbm, g_dst, g_recv.at[core]).start()

    def act_to_y(dx):
        block = chip_at(0, dx)
        for k, dy in ((0, 1), (1, NY - 1)):
            send(acts.at[block], acts.at[block], ay_send.at[dx, k], ay_recv.at[dx, k], peer_at(dy, 0), keep=False)

    def act_to_sib(j):
        block = block_at(j)
        send(acts.at[block], acts.at[block], as_send.at[j], as_recv.at[j], beside, keep=False)

    def act_from_y(dx):
        for k, dy in ((0, NY - 1), (1, 1)):
            block = chip_at(dy, dx)
            got(acts.at[block], ay_recv.at[dx, k])
            send(acts.at[block, k], acts.at[block, k],
                 ah_send.at[dx, k], ah_recv.at[dx, k], peer_at(NY - dy, 0), keep=False)
            act_to_sib(dy * NX + dx)

    def act_halves(dx):
        block = chip_at(2, dx)
        for k in range(2):
            got(acts.at[block, k], ah_recv.at[dx, k])
        act_to_sib(2 * NX + dx)

    def act_from_x():
        got(acts.at[chip_at(0, 1)], ax_sem.at[1])
        act_to_y(1)
        act_to_sib(1)

    cp_w.wait()
    send(wts.at[core], wts.at[core], w_sem.at[0], w_sem.at[1], beside)
    cp_hid.wait()
    act, slp = gelu_parts(hid[...].astype(jnp.float32))
    acts[chip, core] = act.astype(jnp.bfloat16)
    slope[...] = slp
    send(acts.at[chip, core], acts.at[chip, core], own_send, own_recv, beside)

    @pl.when(core == 0)
    def _():
        got(acts.at[chip, 1], own_recv)
        send(acts.at[chip], acts.at[chip], ax_sem.at[0], ax_sem.at[1], peer_at(0, 1), keep=False)
        act_to_y(0)

    pieces = (ch, 1 - ch)

    def right(step, n, par):
        ref = piece(par, rem(cz + NZ - step, NZ), pieces[n])
        if step > 0:
            got(ref, right_recv.at[par, n, step - 1])
        if step < NZ // 2 - n:
            send(ref, ref, right_send.at[par, n, step], right_recv.at[par, n, step], up, keep=False)

    def left(step, n, par):
        ref = piece(par, rem(cz + step, NZ), pieces[n])
        if step > 0:
            got(ref, left_recv.at[par, n, step - 1])
        if step < NZ // 2 - 1 + n:
            send(ref, ref, left_send.at[par, n, step], left_recv.at[par, n, step], down, keep=False)

    def hand(way, step):
        block, half = slot_at(rem(cz + NZ + (step if way else -step), NZ), 0)
        ref = cols.at[0, block, half]
        send(ref, ref, hand_send.at[way, step], hand_recv.at[way, step], beside, keep=False)

    def handed(way, step):
        block, half = slot_at(rem(cz + NZ + (step if way else -step), NZ), 0)
        got(cols.at[0, block, half], hand_recv.at[way, step])

    def ring(step):
        @pl.when(core == 1)
        def _():
            for n in range(2):
                for par in range(2):
                    if step <= NZ // 2 - n:
                        right(step, n, par)
                    if step < NZ // 2 + n:
                        left(step, n, par)
            hand(0, step)
            if step < NZ // 2:
                hand(1, step)

        @pl.when(core == 0)
        def _():
            handed(0, step)
            if step < NZ // 2:
                handed(1, step)

    @pl.when(core == 0)
    def _():
        act_from_x()
        act_from_y(0)
        act_from_y(1)

    @pl.when(core == 1)
    def _():
        for par in range(2):
            ref = piece(par, cz, ch)
            got(ref, g_recv.at[par])
            right(0, 0, par)
            left(0, 0, par)
            send(ref, ref, peer_send.at[par], peer_recv.at[par], across, keep=False)
        for par in range(2):
            got(piece(par, cz, 1 - ch), peer_recv.at[par])
            right(0, 1, par)
            left(0, 1, par)
        hand(0, 0)

    @pl.when(core == 0)
    def _():
        handed(0, 0)

    def partial(step):
        odd = rem(cz + step, 2)
        j = div(rem(cz + NZ + jnp.where(odd == 1, step, -step), NZ), 2)
        dy, dx = shift(j, core)
        block = chip_at(dy, dx)
        j = dy * NX + dx

        @pl.when(core == 1)
        def _():
            ref = cols.at[1, block, 0]
            send(ref, ref, gs_send.at[step - 1], gs_recv.at[block], beside, keep=False)

        if step == 1:
            got(wts.at[1 - core], w_sem.at[1])
        value = jnp.dot(wts[0], cols[core, block, 0], preferred_element_type=jnp.float32)
        value += jnp.dot(wts[1], cols[core, block, 1], preferred_element_type=jnp.float32)
        value = value.astype(jnp.bfloat16)

        @pl.when(j == 0)
        def _():
            parts[0] = value

        @pl.when(j != 0)
        def _():
            stage[step - 1] = value
            send(stage.at[step - 1], parts.at[j], rs_send.at[j], rs_recv.at[j], peer_at(dy, dx), keep=False)

    for step in range(1, NZ // 2 + 1):
        ring(step)
        partial(step)
        if step <= 2:
            @pl.when(core == 0)
            def _():
                act_halves(step - 1)

    @pl.when(core == 1)
    def _():
        got(acts.at[chip, 0], own_recv)
        for j in range(1, NQ):
            got(acts.at[block_at(j)], as_recv.at[j])

    @pl.when(core == 0)
    def _():
        for block in range(NQ):
            got(cols.at[1, block, 0], gs_recv.at[block])

    lhs = jnp.concatenate([cols[par, block, core] for block in range(NQ) for par in range(2)], axis=1)
    total = jnp.dot(lhs, acts[...].reshape(NQ * 256, 768), preferred_element_type=jnp.float32)
    gw_ref[...] = total.astype(jnp.bfloat16)

    for j in range(1, NQ):
        got(parts.at[j], rs_recv.at[j])
    summed = parts[0].astype(jnp.float32)
    for j in range(1, NQ):
        summed += parts[j].astype(jnp.float32)
    gh_ref[...] = (slope[...] * summed.T).astype(jnp.bfloat16)

    @pl.when(to_away)
    def _():
        sent(grad_hbm, g_send)

    @pl.when(core == 1)
    def _():
        ref = piece(0, cz, 0)
        for par in range(2):
            sent(ref, peer_send.at[par])
            for n in range(2):
                for step in range(NZ // 2):
                    if step < NZ // 2 - n:
                        sent(ref, right_send.at[par, n, step])
                    if step < NZ // 2 - 1 + n:
                        sent(ref, left_send.at[par, n, step])
        whole = cols.at[0, 0, 0]
        for step in range(NZ // 2 + 1):
            sent(whole, hand_send.at[0, step])
            if 0 < step < NZ // 2:
                sent(whole, hand_send.at[1, step])
        for step in range(NZ // 2):
            sent(whole, gs_send.at[step])

    for copy in started:
        copy.wait_send()

    @pl.when(core == 0)
    def _():
        sent(acts.at[0], ax_sem.at[0])
        for dx in range(2):
            for k in range(2):
                sent(acts.at[0], ay_send.at[dx, k])
                sent(acts.at[0, 0], ah_send.at[dx, k])
        for j in range(1, NQ):
            sent(acts.at[0], as_send.at[j])

    for j in range(1, NQ):
        sent(stage.at[0], rs_send.at[j])


def local(hidden_pre, out_grad, down_weight):
    bf16, f32 = jnp.bfloat16, jnp.float32
    dma = pltpu.SemaphoreType.DMA
    half = NZ // 2
    grad_hidden, gw = pl.pallas_call(
        kernel,
        out_shape=(
            jax.ShapeDtypeStruct((128, 768), bf16),
            jax.ShapeDtypeStruct((384, 768), bf16),
        ),
        in_specs=[pl.BlockSpec(memory_space=pl.ANY)] * 3,
        out_specs=[pl.BlockSpec(memory_space=pltpu.VMEM)] * 2,
        scratch_shapes=[
            pltpu.VMEM((128, 768), bf16),
            pltpu.VMEM((2, 768, 384), bf16),
            pltpu.VMEM((2, NQ, 2, 384, 128), bf16),
            pltpu.VMEM((NQ, 2, 128, 768), bf16),
            pltpu.VMEM((128, 768), f32),
            pltpu.VMEM((NQ, 768, 128), bf16),
            pltpu.VMEM((NQ, 768, 128), bf16),
            dma((2,)), dma((2,)), dma, dma((2,)), dma((2,)), dma((2,)),
            dma((2, half + 1)), dma((2, half + 1)),
            dma((2, 2, half)), dma((2, 2, half)), dma((2, 2, half)), dma((2, 2, half)),
            dma((half,)), dma((NQ,)), dma, dma, dma((2,)), dma((2, 2)), dma((2, 2)),
            dma((2, 2)), dma((2, 2)), dma((NQ,)), dma((NQ,)),
            dma((NQ,)), dma((NQ,)),
        ],
        compiler_params=pltpu.CompilerParams(
            collective_id=0, has_side_effects=True, vmem_limit_bytes=60 * 1024 * 1024
        ),
    )(hidden_pre, out_grad.T, down_weight)
    return (grad_hidden, gw.T)


def solution(mesh):
    placed = (P("dp", "tensor"), P("dp", "tensor"), P("tensor", "dp"))
    return jax.shard_map(
        local,
        mesh=mesh,
        in_specs=placed,
        out_specs=(P("dp", "tensor"), P("tensor", "dp")),
        check_vma=False,
    )
```

```python
import math

import jax
import jax.numpy as jnp
from jax import lax
from jax.experimental import pallas as pl
from jax.experimental.pallas import tpu as pltpu
from jax.sharding import PartitionSpec as P

coef = math.sqrt(2.0 / math.pi)
MESH = pl.DeviceIdType.MESH
NY, NX, NZ = 4, 2, 16
NQ = NY * NX


def gelu_parts(value):
    inner = coef * (value + 0.044715 * value * value * value)
    tval = jnp.tanh(inner)
    act = 0.5 * value * (1.0 + tval)
    slope = 0.5 * (1.0 + tval) + 0.5 * value * (1.0 - tval * tval) * coef * (
        1.0 + 3.0 * 0.044715 * value * value
    )
    return (act, slope)


def kernel(
    hid_hbm, grad_hbm, w_hbm, gh_ref, gw_ref,
    hid, wts, cols, acts, slope, stage, parts,
    loc_sem, w_sem, g_send, g_recv, peer_send, peer_recv, hand_send, hand_recv, right_send, right_recv, left_send, left_recv,
    gs_send, gs_recv, own_send, own_recv, ax_sem, ay_send, ay_recv, ah_send, ah_recv, as_send, as_recv,
    rs_send, rs_recv,
):
    rem, div = lax.rem, lax.div
    dp = lax.axis_index("dp")
    tn = lax.axis_index("tensor")
    core, chip = rem(dp, 2), div(dp, 2)
    cy, cx = div(chip, NX), rem(chip, NX)
    cz, ch = rem(tn, NZ), div(tn, NZ)
    sib = dp + 1 - 2 * core

    def chip_at(dy, dx):
        return rem(cy + dy, NY) * NX + rem(cx + dx, NX)

    def block_at(j):
        return chip_at(div(j, NX), rem(j, NX))

    def at(dp_to, tn_to):
        return (dp_to, tn_to)

    def peer_at(dy, dx):
        return at(chip_at(dy, dx) * 2 + core, tn)

    def shift(j, par):
        return rem(div(j, NX) + 2 * par, NY), rem(j + par, NX)

    def slot_at(place, par):
        return chip_at(*shift(div(place, 2), par)), rem(place, 2)

    def piece(par, place, part):
        block, half = slot_at(place, par)
        return cols.at[par, block, half, pl.ds(pl.multiple_of(part * 192, 64), 192)]

    to_chip, to_half, to_part = div(tn, 4), rem(div(tn, 2), 2), rem(tn, 2)
    to_j = rem(cy - div(to_chip, NX) + NY + 2 * core, NY) * NX + rem(cx - rem(to_chip, NX) + NX + core, NX)
    to_dp = to_chip * 2 + 1
    to_tn = to_part * NZ + to_j * 2 + to_half
    from_dp = [slot_at(cz, par)[0] * 2 + par for par in range(2)]
    from_tn = chip * 4 + rem(cz, 2) * 2 + ch
    to_away = jnp.logical_or(to_dp != dp, to_tn != tn)

    up = at(dp, ch * NZ + rem(cz + 1, NZ))
    down = at(dp, ch * NZ + rem(cz + NZ - 1, NZ))
    across = at(dp, rem(tn + NZ, 2 * NZ))
    beside = at(sib, tn)

    barrier = pltpu.get_barrier_semaphore()
    @pl.when(core == 1)
    def _():
        pl.semaphore_signal(barrier, inc=1, device_id=at(from_dp[0], from_tn), device_id_type=MESH)

        @pl.when(jnp.logical_or(from_dp[1] != dp, from_tn != tn))
        def _():
            pl.semaphore_signal(barrier, inc=1, device_id=at(from_dp[1], from_tn), device_id_type=MESH)

        for other in (up, down, across):
            pl.semaphore_signal(barrier, inc=1, device_id=other, device_id_type=MESH)

    greet = [beside] + [peer_at(j // NX, j % NX) for j in range(1, NQ)]
    for other in greet:
        pl.semaphore_signal(barrier, inc=1, device_id=other, device_id_type=MESH)

    cp_hid = pltpu.make_async_copy(hid_hbm, hid, loc_sem.at[0])
    cp_w = pltpu.make_async_copy(w_hbm, wts.at[core], loc_sem.at[1])
    cp_hid.start()
    cp_w.start()
    pl.semaphore_wait(barrier, len(greet) + 3 * core + to_away.astype(jnp.int32))

    started = []

    def send(src, dst, send_sem, recv_sem, dest, keep=True):
        copy = pltpu.make_async_remote_copy(
            src_ref=src, dst_ref=dst, send_sem=send_sem, recv_sem=recv_sem,
            device_id=dest, device_id_type=MESH,
        )
        copy.start()
        if keep:
            started.append(copy)

    def got(dst, recv_sem):
        pltpu.make_async_remote_copy(
            src_ref=dst, dst_ref=dst, send_sem=recv_sem, recv_sem=recv_sem,
            device_id=beside, device_id_type=MESH,
        ).wait_recv()

    def sent(src, send_sem):
        pltpu.make_async_remote_copy(
            src_ref=src, dst_ref=src, send_sem=send_sem, recv_sem=send_sem,
            device_id=beside, device_id_type=MESH,
        ).wait_send()

    g_dst = cols.at[core, chip, to_half, pl.ds(pl.multiple_of(to_part * 192, 64), 192)]

    @pl.when(to_away)
    def _():
        send(grad_hbm, g_dst, g_send, g_recv.at[core], at(to_dp, to_tn), keep=False)

    @pl.when(jnp.logical_not(to_away))
    def _():
        pltpu.make_async_copy(grad_hbm, g_dst, g_recv.at[core]).start()

    def act_to_y(dx):
        block = chip_at(0, dx)
        for k, dy in ((0, 1), (1, NY - 1)):
            send(acts.at[block], acts.at[block], ay_send.at[dx, k], ay_recv.at[dx, k], peer_at(dy, 0), keep=False)

    def act_to_sib(j):
        block = block_at(j)
        send(acts.at[block], acts.at[block], as_send.at[j], as_recv.at[j], beside, keep=False)

    def act_from_y(dx):
        for k, dy in ((0, NY - 1), (1, 1)):
            block = chip_at(dy, dx)
            got(acts.at[block], ay_recv.at[dx, k])
            send(acts.at[block, k], acts.at[block, k],
                 ah_send.at[dx, k], ah_recv.at[dx, k], peer_at(NY - dy, 0), keep=False)
            act_to_sib(dy * NX + dx)

    def act_halves(dx):
        block = chip_at(2, dx)
        for k in range(2):
            got(acts.at[block, k], ah_recv.at[dx, k])
        act_to_sib(2 * NX + dx)

    def act_from_x():
        got(acts.at[chip_at(0, 1)], ax_sem.at[1])
        act_to_y(1)
        act_to_sib(1)

    cp_hid.wait()
    acts[chip, core] = gelu_parts(hid[...].astype(jnp.float32))[0].astype(jnp.bfloat16)
    send(acts.at[chip, core], acts.at[chip, core], own_send, own_recv, beside)
    cp_w.wait()

    @pl.when(core == 0)
    def _():
        got(acts.at[chip, 1], own_recv)
        send(acts.at[chip], acts.at[chip], ax_sem.at[0], ax_sem.at[1], peer_at(0, 1), keep=False)
        act_to_y(0)

    send(wts.at[core], wts.at[core], w_sem.at[0], w_sem.at[1], beside)
    slope[...] = gelu_parts(hid[...].astype(jnp.float32))[1]

    pieces = (ch, 1 - ch)

    def right(step, n, par):
        ref = piece(par, rem(cz + NZ - step, NZ), pieces[n])
        if step > 0:
            got(ref, right_recv.at[par, n, step - 1])
        if step < NZ // 2 - n:
            send(ref, ref, right_send.at[par, n, step], right_recv.at[par, n, step], up, keep=False)

    def left(step, n, par):
        ref = piece(par, rem(cz + step, NZ), pieces[n])
        if step > 0:
            got(ref, left_recv.at[par, n, step - 1])
        if step < NZ // 2 - 1 + n:
            send(ref, ref, left_send.at[par, n, step], left_recv.at[par, n, step], down, keep=False)

    def hand(way, step):
        block, half = slot_at(rem(cz + NZ + (step if way else -step), NZ), 0)
        ref = cols.at[0, block, half]
        send(ref, ref, hand_send.at[way, step], hand_recv.at[way, step], beside, keep=False)

    def handed(way, step):
        block, half = slot_at(rem(cz + NZ + (step if way else -step), NZ), 0)
        got(cols.at[0, block, half], hand_recv.at[way, step])

    def ring(step):
        @pl.when(core == 1)
        def _():
            for n in range(2):
                for par in range(2):
                    if step <= NZ // 2 - n:
                        right(step, n, par)
                    if step < NZ // 2 + n:
                        left(step, n, par)
            hand(0, step)
            if step < NZ // 2:
                hand(1, step)

        @pl.when(core == 0)
        def _():
            handed(0, step)
            if step < NZ // 2:
                handed(1, step)

    @pl.when(core == 0)
    def _():
        act_from_x()
        act_from_y(0)
        act_from_y(1)

    @pl.when(core == 1)
    def _():
        for par in range(2):
            ref = piece(par, cz, ch)
            got(ref, g_recv.at[par])
            right(0, 0, par)
            left(0, 0, par)
            send(ref, ref, peer_send.at[par], peer_recv.at[par], across, keep=False)
        for par in range(2):
            got(piece(par, cz, 1 - ch), peer_recv.at[par])
            right(0, 1, par)
            left(0, 1, par)
        hand(0, 0)

    @pl.when(core == 0)
    def _():
        handed(0, 0)

    def partial(step):
        odd = rem(cz + step, 2)
        j = div(rem(cz + NZ + jnp.where(odd == 1, step, -step), NZ), 2)
        dy, dx = shift(j, core)
        block = chip_at(dy, dx)
        j = dy * NX + dx

        @pl.when(core == 1)
        def _():
            ref = cols.at[1, block, 0]
            send(ref, ref, gs_send.at[step - 1], gs_recv.at[block], beside, keep=False)

        if step == 1:
            got(wts.at[1 - core], w_sem.at[1])
        rows = 384 if step == NZ // 2 else 768
        for at_row in range(0, 768, rows):
            some = pl.ds(at_row, rows)
            value = jnp.dot(wts[0, some], cols[core, block, 0], preferred_element_type=jnp.float32)
            value += jnp.dot(wts[1, some], cols[core, block, 1], preferred_element_type=jnp.float32)
            value = value.astype(jnp.bfloat16)

            @pl.when(j == 0)
            def _():
                parts[0, some] = value

            @pl.when(j != 0)
            def _():
                stage[step - 1, some] = value
                send(stage.at[step - 1, some], parts.at[j, some], rs_send.at[j], rs_recv.at[j],
                     peer_at(dy, dx), keep=False)

    for step in range(1, NZ // 2 + 1):
        ring(step)
        partial(step)
        if step <= 2:
            @pl.when(core == 0)
            def _():
                act_halves(step - 1)

    @pl.when(core == 1)
    def _():
        got(acts.at[chip, 0], own_recv)
        for j in range(1, NQ):
            got(acts.at[block_at(j)], as_recv.at[j])

    @pl.when(core == 0)
    def _():
        for block in range(NQ):
            got(cols.at[1, block, 0], gs_recv.at[block])

    lhs = jnp.concatenate([cols[par, block, core] for block in range(NQ) for par in range(2)], axis=1)
    total = jnp.dot(lhs, acts[...].reshape(NQ * 256, 768), preferred_element_type=jnp.float32)
    gw_ref[...] = total.astype(jnp.bfloat16)

    for j in range(1, NQ):
        got(parts.at[j], rs_recv.at[j])
    summed = parts[0].astype(jnp.float32)
    for j in range(1, NQ):
        summed += parts[j].astype(jnp.float32)
    gh_ref[...] = (slope[...] * summed.T).astype(jnp.bfloat16)

    @pl.when(to_away)
    def _():
        sent(grad_hbm, g_send)

    @pl.when(core == 1)
    def _():
        ref = piece(0, cz, 0)
        for par in range(2):
            sent(ref, peer_send.at[par])
            for n in range(2):
                for step in range(NZ // 2):
                    if step < NZ // 2 - n:
                        sent(ref, right_send.at[par, n, step])
                    if step < NZ // 2 - 1 + n:
                        sent(ref, left_send.at[par, n, step])
        whole = cols.at[0, 0, 0]
        for step in range(NZ // 2 + 1):
            sent(whole, hand_send.at[0, step])
            if 0 < step < NZ // 2:
                sent(whole, hand_send.at[1, step])
        for step in range(NZ // 2):
            sent(whole, gs_send.at[step])

    for copy in started:
        copy.wait_send()

    @pl.when(core == 0)
    def _():
        sent(acts.at[0], ax_sem.at[0])
        for dx in range(2):
            for k in range(2):
                sent(acts.at[0], ay_send.at[dx, k])
                sent(acts.at[0, 0], ah_send.at[dx, k])
        for j in range(1, NQ):
            sent(acts.at[0], as_send.at[j])

    for j in range(1, NQ):
        sent(stage.at[0], rs_send.at[j])


def local(hidden_pre, out_grad, down_weight):
    bf16, f32 = jnp.bfloat16, jnp.float32
    dma = pltpu.SemaphoreType.DMA
    half = NZ // 2
    grad_hidden, gw = pl.pallas_call(
        kernel,
        out_shape=(
            jax.ShapeDtypeStruct((128, 768), bf16),
            jax.ShapeDtypeStruct((384, 768), bf16),
        ),
        in_specs=[pl.BlockSpec(memory_space=pl.ANY)] * 3,
        out_specs=[pl.BlockSpec(memory_space=pltpu.VMEM)] * 2,
        scratch_shapes=[
            pltpu.VMEM((128, 768), bf16),
            pltpu.VMEM((2, 768, 384), bf16),
            pltpu.VMEM((2, NQ, 2, 384, 128), bf16),
            pltpu.VMEM((NQ, 2, 128, 768), bf16),
            pltpu.VMEM((128, 768), f32),
            pltpu.VMEM((NQ, 768, 128), bf16),
            pltpu.VMEM((NQ, 768, 128), bf16),
            dma((2,)), dma((2,)), dma, dma((2,)), dma((2,)), dma((2,)),
            dma((2, half + 1)), dma((2, half + 1)),
            dma((2, 2, half)), dma((2, 2, half)), dma((2, 2, half)), dma((2, 2, half)),
            dma((half,)), dma((NQ,)), dma, dma, dma((2,)), dma((2, 2)), dma((2, 2)),
            dma((2, 2)), dma((2, 2)), dma((NQ,)), dma((NQ,)),
            dma((NQ,)), dma((NQ,)),
        ],
        compiler_params=pltpu.CompilerParams(
            collective_id=0, has_side_effects=True, vmem_limit_bytes=60 * 1024 * 1024
        ),
    )(hidden_pre, out_grad.T, down_weight)
    return (grad_hidden, gw.T)


def solution(mesh):
    placed = (P("dp", "tensor"), P("dp", "tensor"), P("tensor", "dp"))
    return jax.shard_map(
        local,
        mesh=mesh,
        in_specs=placed,
        out_specs=(P("dp", "tensor"), P("tensor", "dp")),
        check_vma=False,
    )
```

```python
import math

import jax
import jax.numpy as jnp
from jax import lax
from jax.experimental import pallas as pl
from jax.experimental.pallas import tpu as pltpu
from jax.sharding import PartitionSpec as P

coef = math.sqrt(2.0 / math.pi)
MESH = pl.DeviceIdType.MESH
NY, NX, NZ = 4, 2, 16
NQ = NY * NX


def gelu_parts(value):
    inner = coef * (value + 0.044715 * value * value * value)
    tval = jnp.tanh(inner)
    act = 0.5 * value * (1.0 + tval)
    slope = 0.5 * (1.0 + tval) + 0.5 * value * (1.0 - tval * tval) * coef * (
        1.0 + 3.0 * 0.044715 * value * value
    )
    return (act, slope)


def kernel(
    hid_hbm, grad_hbm, w_hbm, gh_ref, gw_ref,
    hid, wts, cols, acts, slope, stage, parts,
    loc_sem, w_sem, g_send, g_recv, peer_send, peer_recv, hand_send, hand_recv, right_send, right_recv, left_send, left_recv,
    gs_send, gs_recv, own_send, own_recv, ax_sem, ay_send, ay_recv, ah_send, ah_recv, as_send, as_recv,
    rs_send, rs_recv,
):
    rem, div = lax.rem, lax.div
    dp = lax.axis_index("dp")
    tn = lax.axis_index("tensor")
    core, chip = rem(dp, 2), div(dp, 2)
    cy, cx = div(chip, NX), rem(chip, NX)
    cz, ch = rem(tn, NZ), div(tn, NZ)
    sib = dp + 1 - 2 * core

    def chip_at(dy, dx):
        return rem(cy + dy, NY) * NX + rem(cx + dx, NX)

    def block_at(j):
        return chip_at(div(j, NX), rem(j, NX))

    def at(dp_to, tn_to):
        return (dp_to, tn_to)

    def peer_at(dy, dx):
        return at(chip_at(dy, dx) * 2 + core, tn)

    def shift(j, par):
        return rem(div(j, NX) + 2 * par, NY), rem(j + par, NX)

    def turned(place, y):
        return rem(place + 6 + 8 * rem(y, 2), NZ)

    def slot_at(place, par):
        return chip_at(*shift(div(turned(place, cy), 2), par)), rem(place, 2)

    def piece(par, place, part):
        block, half = slot_at(place, par)
        return cols.at[par, block, half, pl.ds(pl.multiple_of(part * 192, 64), 192)]

    to_chip, to_half, to_part = div(tn, 4), rem(div(tn, 2), 2), rem(tn, 2)
    to_j = rem(cy - div(to_chip, NX) + NY + 2 * core, NY) * NX + rem(cx - rem(to_chip, NX) + NX + core, NX)
    to_dp = to_chip * 2 + 1
    to_z = rem(to_j * 2 + to_half + 2 + 8 * rem(div(to_chip, NX) + 1, 2), NZ)
    to_tn = to_part * NZ + to_z
    from_dp = [slot_at(cz, par)[0] * 2 + par for par in range(2)]
    from_tn = chip * 4 + rem(cz, 2) * 2 + ch
    to_away = jnp.logical_or(to_dp != dp, to_tn != tn)

    up = at(dp, ch * NZ + rem(cz + 1, NZ))
    down = at(dp, ch * NZ + rem(cz + NZ - 1, NZ))
    across = at(dp, rem(tn + NZ, 2 * NZ))
    beside = at(sib, tn)

    barrier = pltpu.get_barrier_semaphore()
    @pl.when(core == 1)
    def _():
        pl.semaphore_signal(barrier, inc=1, device_id=at(from_dp[0], from_tn), device_id_type=MESH)

        @pl.when(jnp.logical_or(from_dp[1] != dp, from_tn != tn))
        def _():
            pl.semaphore_signal(barrier, inc=1, device_id=at(from_dp[1], from_tn), device_id_type=MESH)

        for other in (up, down, across):
            pl.semaphore_signal(barrier, inc=1, device_id=other, device_id_type=MESH)

    greet = [beside] + [peer_at(j // NX, j % NX) for j in range(1, NQ)]
    for other in greet:
        pl.semaphore_signal(barrier, inc=1, device_id=other, device_id_type=MESH)

    cp_hid = pltpu.make_async_copy(hid_hbm, hid, loc_sem.at[0])
    cp_w = pltpu.make_async_copy(w_hbm, wts.at[core], loc_sem.at[1])
    cp_hid.start()
    cp_w.start()
    pl.semaphore_wait(barrier, len(greet) + 3 * core + to_away.astype(jnp.int32))

    started = []

    def send(src, dst, send_sem, recv_sem, dest, keep=True):
        copy = pltpu.make_async_remote_copy(
            src_ref=src, dst_ref=dst, send_sem=send_sem, recv_sem=recv_sem,
            device_id=dest, device_id_type=MESH,
        )
        copy.start()
        if keep:
            started.append(copy)

    def got(dst, recv_sem):
        pltpu.make_async_remote_copy(
            src_ref=dst, dst_ref=dst, send_sem=recv_sem, recv_sem=recv_sem,
            device_id=beside, device_id_type=MESH,
        ).wait_recv()

    def sent(src, send_sem):
        pltpu.make_async_remote_copy(
            src_ref=src, dst_ref=src, send_sem=send_sem, recv_sem=send_sem,
            device_id=beside, device_id_type=MESH,
        ).wait_send()

    g_dst = cols.at[core, chip, to_half, pl.ds(pl.multiple_of(to_part * 192, 64), 192)]

    @pl.when(to_away)
    def _():
        send(grad_hbm, g_dst, g_send, g_recv.at[core], at(to_dp, to_tn), keep=False)

    @pl.when(jnp.logical_not(to_away))
    def _():
        pltpu.make_async_copy(grad_hbm, g_dst, g_recv.at[core]).start()

    def act_to_y(dx):
        block = chip_at(0, dx)
        for k, dy in ((0, 1), (1, NY - 1)):
            send(acts.at[block], acts.at[block], ay_send.at[dx, k], ay_recv.at[dx, k], peer_at(dy, 0), keep=False)

    def act_to_sib(j):
        block = block_at(j)
        send(acts.at[block], acts.at[block], as_send.at[j], as_recv.at[j], beside, keep=False)

    def act_from_y(dx):
        for k, dy in ((0, NY - 1), (1, 1)):
            block = chip_at(dy, dx)
            got(acts.at[block], ay_recv.at[dx, k])
            send(acts.at[block, k], acts.at[block, k],
                 ah_send.at[dx, k], ah_recv.at[dx, k], peer_at(NY - dy, 0), keep=False)
            act_to_sib(dy * NX + dx)

    def act_halves(dx):
        block = chip_at(2, dx)
        for k in range(2):
            got(acts.at[block, k], ah_recv.at[dx, k])
        act_to_sib(2 * NX + dx)

    def act_from_x():
        got(acts.at[chip_at(0, 1)], ax_sem.at[1])
        act_to_y(1)
        act_to_sib(1)

    cp_w.wait()
    send(wts.at[core], wts.at[core], w_sem.at[0], w_sem.at[1], beside)
    cp_hid.wait()
    act, slp = gelu_parts(hid[...].astype(jnp.float32))
    acts[chip, core] = act.astype(jnp.bfloat16)
    slope[...] = slp
    send(acts.at[chip, core], acts.at[chip, core], own_send, own_recv, beside)

    @pl.when(core == 0)
    def _():
        got(acts.at[chip, 1], own_recv)
        send(acts.at[chip], acts.at[chip], ax_sem.at[0], ax_sem.at[1], peer_at(0, 1), keep=False)
        act_to_y(0)

    pieces = (ch, 1 - ch)

    def right(step, n, par):
        ref = piece(par, rem(cz + NZ - step, NZ), pieces[n])
        if step > 0:
            got(ref, right_recv.at[par, n, step - 1])
        if step < NZ // 2 - n:
            send(ref, ref, right_send.at[par, n, step], right_recv.at[par, n, step], up, keep=False)

    def left(step, n, par):
        ref = piece(par, rem(cz + step, NZ), pieces[n])
        if step > 0:
            got(ref, left_recv.at[par, n, step - 1])
        if step < NZ // 2 - 1 + n:
            send(ref, ref, left_send.at[par, n, step], left_recv.at[par, n, step], down, keep=False)

    def hand(way, step):
        block, half = slot_at(rem(cz + NZ + (step if way else -step), NZ), 0)
        ref = cols.at[0, block, half]
        send(ref, ref, hand_send.at[way, step], hand_recv.at[way, step], beside, keep=False)

    def handed(way, step):
        block, half = slot_at(rem(cz + NZ + (step if way else -step), NZ), 0)
        got(cols.at[0, block, half], hand_recv.at[way, step])

    def ring(step):
        @pl.when(core == 1)
        def _():
            for n in range(2):
                for par in range(2):
                    if step <= NZ // 2 - n:
                        right(step, n, par)
                    if step < NZ // 2 + n:
                        left(step, n, par)
            hand(0, step)
            if step < NZ // 2:
                hand(1, step)

        @pl.when(core == 0)
        def _():
            handed(0, step)
            if step < NZ // 2:
                handed(1, step)

    @pl.when(core == 0)
    def _():
        act_from_x()
        act_from_y(0)
        act_from_y(1)

    @pl.when(core == 1)
    def _():
        for par in range(2):
            ref = piece(par, cz, ch)
            got(ref, g_recv.at[par])
            right(0, 0, par)
            left(0, 0, par)
            send(ref, ref, peer_send.at[par], peer_recv.at[par], across, keep=False)
        for par in range(2):
            got(piece(par, cz, 1 - ch), peer_recv.at[par])
            right(0, 1, par)
            left(0, 1, par)
        hand(0, 0)

    @pl.when(core == 0)
    def _():
        handed(0, 0)

    def partial(step):
        odd = rem(cz + step, 2)
        j = div(turned(rem(cz + NZ + jnp.where(odd == 1, step, -step), NZ), cy), 2)
        dy, dx = shift(j, core)
        block = chip_at(dy, dx)
        j = dy * NX + dx

        @pl.when(core == 1)
        def _():
            ref = cols.at[1, block, 0]
            send(ref, ref, gs_send.at[step - 1], gs_recv.at[block], beside, keep=False)

        if step == 1:
            got(wts.at[1 - core], w_sem.at[1])
        value = jnp.dot(wts[0], cols[core, block, 0], preferred_element_type=jnp.float32)
        value += jnp.dot(wts[1], cols[core, block, 1], preferred_element_type=jnp.float32)
        value = value.astype(jnp.bfloat16)

        @pl.when(j == 0)
        def _():
            parts[0] = value

        @pl.when(j != 0)
        def _():
            stage[step - 1] = value
            send(stage.at[step - 1], parts.at[j], rs_send.at[j], rs_recv.at[j], peer_at(dy, dx), keep=False)

    for step in range(1, NZ // 2 + 1):
        ring(step)
        partial(step)
        if step <= 2:
            @pl.when(core == 0)
            def _():
                act_halves(step - 1)

    @pl.when(core == 1)
    def _():
        got(acts.at[chip, 0], own_recv)
        for j in range(1, NQ):
            got(acts.at[block_at(j)], as_recv.at[j])

    @pl.when(core == 0)
    def _():
        for block in range(NQ):
            got(cols.at[1, block, 0], gs_recv.at[block])

    lhs = jnp.concatenate([cols[par, block, core] for block in range(NQ) for par in range(2)], axis=1)
    total = jnp.dot(lhs, acts[...].reshape(NQ * 256, 768), preferred_element_type=jnp.float32)
    gw_ref[...] = total.astype(jnp.bfloat16)

    for j in range(1, NQ):
        got(parts.at[j], rs_recv.at[j])
    summed = parts[0].astype(jnp.float32)
    for j in range(1, NQ):
        summed += parts[j].astype(jnp.float32)
    gh_ref[...] = (slope[...] * summed.T).astype(jnp.bfloat16)

    @pl.when(to_away)
    def _():
        sent(grad_hbm, g_send)

    @pl.when(core == 1)
    def _():
        ref = piece(0, cz, 0)
        for par in range(2):
            sent(ref, peer_send.at[par])
            for n in range(2):
                for step in range(NZ // 2):
                    if step < NZ // 2 - n:
                        sent(ref, right_send.at[par, n, step])
                    if step < NZ // 2 - 1 + n:
                        sent(ref, left_send.at[par, n, step])
        whole = cols.at[0, 0, 0]
        for step in range(NZ // 2 + 1):
            sent(whole, hand_send.at[0, step])
            if 0 < step < NZ // 2:
                sent(whole, hand_send.at[1, step])
        for step in range(NZ // 2):
            sent(whole, gs_send.at[step])

    for copy in started:
        copy.wait_send()

    @pl.when(core == 0)
    def _():
        sent(acts.at[0], ax_sem.at[0])
        for dx in range(2):
            for k in range(2):
                sent(acts.at[0], ay_send.at[dx, k])
                sent(acts.at[0, 0], ah_send.at[dx, k])
        for j in range(1, NQ):
            sent(acts.at[0], as_send.at[j])

    for j in range(1, NQ):
        sent(stage.at[0], rs_send.at[j])


def local(hidden_pre, out_grad, down_weight):
    bf16, f32 = jnp.bfloat16, jnp.float32
    dma = pltpu.SemaphoreType.DMA
    half = NZ // 2
    grad_hidden, gw = pl.pallas_call(
        kernel,
        out_shape=(
            jax.ShapeDtypeStruct((128, 768), bf16),
            jax.ShapeDtypeStruct((384, 768), bf16),
        ),
        in_specs=[pl.BlockSpec(memory_space=pl.ANY)] * 3,
        out_specs=[pl.BlockSpec(memory_space=pltpu.VMEM)] * 2,
        scratch_shapes=[
            pltpu.VMEM((128, 768), bf16),
            pltpu.VMEM((2, 768, 384), bf16),
            pltpu.VMEM((2, NQ, 2, 384, 128), bf16),
            pltpu.VMEM((NQ, 2, 128, 768), bf16),
            pltpu.VMEM((128, 768), f32),
            pltpu.VMEM((NQ, 768, 128), bf16),
            pltpu.VMEM((NQ, 768, 128), bf16),
            dma((2,)), dma((2,)), dma, dma((2,)), dma((2,)), dma((2,)),
            dma((2, half + 1)), dma((2, half + 1)),
            dma((2, 2, half)), dma((2, 2, half)), dma((2, 2, half)), dma((2, 2, half)),
            dma((half,)), dma((NQ,)), dma, dma, dma((2,)), dma((2, 2)), dma((2, 2)),
            dma((2, 2)), dma((2, 2)), dma((NQ,)), dma((NQ,)),
            dma((NQ,)), dma((NQ,)),
        ],
        compiler_params=pltpu.CompilerParams(
            collective_id=0, has_side_effects=True, vmem_limit_bytes=60 * 1024 * 1024
        ),
    )(hidden_pre, out_grad.T, down_weight)
    return (grad_hidden, gw.T)


def solution(mesh):
    placed = (P("dp", "tensor"), P("dp", "tensor"), P("tensor", "dp"))
    return jax.shard_map(
        local,
        mesh=mesh,
        in_specs=placed,
        out_specs=(P("dp", "tensor"), P("tensor", "dp")),
        check_vma=False,
    )
```
